256 devices in a mesh: tile: 32 (over z, x), ens: 8 (over y, core).
Axes of the slice: x: 4, y: 4, z: 8, core: 2. Of those that a mesh axis runs over, the one named last changes fastest.
Arguments:
- perturbations: bfloat16 [80, 16, 512, 128], P('ens', None, 'tile'), may hold values from -9 to 9
- innovations: float32 [65536], P('tile'), may hold values from -48 to 48
- obs_precision: float32 [65536], P('tile'), may hold values from 0.001 to 0.016
- obs_weights: float32 [16, 65536], P(None, 'tile'), may hold values from -1.5 to 1.5
- obs_cell: int32 [65536], P('tile'), may hold values from 0 to 2047
- obs_count: int32 [32], P('tile'), may hold values from 1 to 2048, as said below
Outputs:
- alpha_fields: float32 [80, 16, 512, 128], P('ens', None, 'tile')
- increment: float32 [16, 512, 128], P(None, 'tile')
The draws below stay inside these ranges and needn't reach their ends.
Inputs may be any that keep to these rules, and one draw needn't show every extreme that they name: Tile t's observations fill slots 0 to obs_count[t] - 1 of its 2048 slots; the other slots are ignored; in every draw some tile is full. `obs_cell`: A cell of a tile is numbered x * 128 + y with x its row within the tile.
All inputs are finite; a program needn't handle non-finite values.
Results may differ from the reference program's by a relative error of at most 0.0004.
Values may be sent and summed in bfloat16 or wider, within the bound.
No kernel may reach another device: no remote copies, remote signals or barrier semaphores. Data moves between devices by JAX's collectives and lax.ppermute only.
A program may use at most 64 MiB of HBM per device.

```python
import math
import jax
import jax.numpy as jnp
from jax import lax

GX = 16
GY = 128
LEVELS = 16
OBS_CAP = 2048
ITERS = 2
HALO = 8
MEMBERS = 80
TILES = 32
NX = 512
TILE_OBS = 65536


def draw_obs_count(key, part):
    key = jax.random.fold_in(key, 11)
    key_count, key_full = jax.random.split(key)
    drawn_root = jax.random.randint(key_count, (TILES,), 0, 256)
    counts = 1 + drawn_root * drawn_root * (OBS_CAP - 1) // 65025
    fullest = jax.random.randint(key_full, (), 0, TILES)
    return jnp.where(jnp.arange(TILES) == fullest, OBS_CAP, counts).astype(jnp.int32)


def plant(values, own_key, smallest, largest):
    longest = values.shape.index(max(values.shape))
    spots = []
    for shift in (0, 1):
        where = [jax.random.randint(jax.random.fold_in(own_key, axis), (), 0, length) for axis, length in enumerate(values.shape)]
        where[longest] = (where[longest] + shift) % values.shape[longest]
        spots.append(tuple(where))
    return values.at[spots[0]].set(smallest).at[spots[1]].set(largest)


def block_levels(key, shape, shards, least, top_value):
    factor_of = 1.0
    for dim, shards_of in shards:
        heights = jax.random.uniform(jax.random.fold_in(jax.random.fold_in(key, 6), dim), (shards_of,), jnp.float32, least / len(shards), top_value / len(shards))
        factor_of = factor_of * jnp.repeat(jnp.exp(heights), shape[dim] // shards_of).reshape((-1,) + (1,) * (len(shape) - 1 - dim))
    return factor_of


def scatter_about(key, shape, width, bound, cuts=(), kind=jnp.bfloat16):
    values = width * jax.random.normal(key, shape, jnp.float32)
    if cuts:
        values = values * block_levels(key, shape, cuts, -0.22, 0.18)
    return jnp.clip(values, -bound, bound).astype(kind)


def setup_inputs(seed: int = 0) -> dict:
    seeds = jax.random.split(jax.random.key(seed), 7)
    return {
        "perturbations": scatter_about(seeds[0], (MEMBERS, LEVELS, NX, GY), 3.0, 9.0, ((0, 8), (2, 32))),
        "innovations": scatter_about(seeds[1], (TILE_OBS,), 8.0, 48.0, ((0, 32),), jnp.float32),
        "obs_precision": jnp.clip(jnp.exp(math.log(0.016) - 2.7725887 * jax.random.uniform(seeds[2], (TILE_OBS,), jnp.float32) ** block_levels(seeds[2], (TILE_OBS,), ((0, 32),), -0.2, 0.2)), 0.001, 0.016),
        "obs_weights": scatter_about(seeds[3], (LEVELS, TILE_OBS), LEVELS ** -0.5, 1.5, ((1, 32),), jnp.float32),
        "obs_cell": plant(jax.random.randint(seeds[4], (TILE_OBS,), 0, GX * GY), jax.random.fold_in(seeds[4], 1), 0, (GX * GY) - 1).astype(jnp.int32),
        "obs_count": draw_obs_count(jax.random.fold_in(seeds[6], 71), 0),
    }


highest = lax.Precision.HIGHEST
vertical_spread = 2.0

def gauss_kernel(radius, spread):
    offsets = jnp.arange(-radius, radius + 1).astype(jnp.float32) / spread
    return jnp.exp(-offsets * offsets)

def x_kernel(radius):
    kernel = gauss_kernel(radius, float(radius))
    return kernel / jnp.sqrt(jnp.sum(kernel * kernel))

def band_matrix(length, spread):
    position = jnp.arange(length).astype(jnp.float32)
    spacing = (position[:, None] - position[None, :]) / spread
    entire = gauss_kernel(length, spread)
    return jnp.exp(-spacing * spacing) / jnp.sqrt(jnp.sum(entire * entire))

def reference(perturbations, innovations, obs_precision, obs_weights, obs_cell, obs_count):
    vertical = band_matrix(LEVELS, vertical_spread)
    lateral = band_matrix(GY, GY / 16.0)
    kernel = x_kernel(HALO)
    scale = 1.0 / math.sqrt(MEMBERS)
    slots = jnp.arange(TILES * OBS_CAP).astype(jnp.int32)
    tile_of = slots // OBS_CAP
    live_mask = (slots % OBS_CAP < obs_count[tile_of]).astype(jnp.float32)
    row_at = tile_of * GX + obs_cell // GY
    column_at = obs_cell % GY

    def localize_member(field):
        field = jnp.einsum('lm,mxy->lxy', vertical, field, precision=highest)
        field = jnp.einsum('lxy,yb->lxb', field, lateral, precision=highest)
        result = jnp.zeros_like(field)
        for offset in range(-HALO, HALO + 1):
            result = result + kernel[offset + HALO] * jnp.roll(field, -offset, axis=1)
        return result

    def increment_of(fields):

        def accumulate(carry, paired):
            member, field = paired
            return (carry + member.astype(jnp.float32) * localize_member(field), None)
        start = jnp.zeros((LEVELS, NX, GY), jnp.float32)
        summed, unused = lax.scan(accumulate, start, (perturbations, fields))
        return summed * scale

    def observe(field):
        picked = field[:, row_at, column_at]
        return live_mask * lax.optimization_barrier(jnp.sum(obs_weights * picked, axis=0))

    def observe_adjoint(values):
        addition = obs_weights * (live_mask * values)[None, :]
        return jnp.zeros((LEVELS, NX, GY), jnp.float32).at[:, row_at, column_at].add(addition)

    def adjoint_localize(gradient):
        return lax.map(lambda member: localize_member(member.astype(jnp.float32) * gradient * scale), perturbations)

    def hessian(direction):
        gradient = observe_adjoint(obs_precision * observe(increment_of(direction)))
        return direction + adjoint_localize(gradient)
    right_side = adjoint_localize(observe_adjoint(obs_precision * innovations))
    solution = jnp.zeros_like(right_side)
    residual = right_side
    direction = right_side
    norm_now = jnp.sum(residual * residual)
    for iteration in range(ITERS):
        applied = hessian(direction)
        step_size = norm_now / jnp.sum(direction * applied)
        solution = solution + step_size * direction
        residual = residual - step_size * applied
        norm_next = jnp.sum(residual * residual)
        direction = residual + norm_next / norm_now * direction
        norm_now = norm_next
    return (solution, increment_of(solution))
```

```python
import math

import jax
import jax.numpy as jnp
import numpy as np
from jax import lax
from jax.experimental import pallas as pl
from jax.experimental.pallas import tpu as pltpu
from jax.sharding import PartitionSpec as P

F32 = jnp.float32
BF16 = jnp.bfloat16
VERTICAL_SPREAD = 2.0
VMEM_LIMIT = 40 * 1024 * 1024


def gauss(radius, spread):
    offsets = np.arange(-radius, radius + 1) / spread
    return np.exp(-offsets * offsets)


def band(length, spread):
    position = np.arange(length)
    spacing = (position[:, None] - position[None, :]) / spread
    return np.exp(-spacing * spacing) / np.sqrt(np.sum(gauss(length, spread) ** 2))


def bf16_pair(matrix):
    matrix = matrix.astype(np.float32)
    high = matrix.astype(jnp.bfloat16)
    low = (matrix - high.astype(np.float32)).astype(jnp.bfloat16)
    return high, low


def local_matrices(levels, rows, columns, power, scale):
    radius = rows // 2
    kernel = gauss(radius, float(radius))
    kernel = kernel / np.sqrt(np.sum(kernel * kernel))
    vertical = band(levels, VERTICAL_SPREAD)
    lateral = band(columns, columns / 16.0)
    if power == 2:
        kernel = np.convolve(kernel, kernel)
        vertical = vertical @ vertical
        lateral = lateral @ lateral
    reach = (len(kernel) - 1) // 2
    blocks = []
    for tile in (-1, 0, 1):
        offset = tile * rows + np.arange(rows)[None, :] - np.arange(rows)[:, None]
        inside = np.abs(offset) <= reach
        along = np.where(inside, kernel[np.clip(offset + reach, 0, 2 * reach)], 0.0)
        blocks.append(np.kron(vertical, along))
    rows_high, rows_low = bf16_pair(np.concatenate(blocks, axis=1) * scale)
    pair_high, pair_low = bf16_pair(np.kron(np.eye(2), lateral))
    return np.concatenate([rows_high, rows_low], axis=0), pair_high, pair_low


def split(x):
    high = x.astype(BF16)
    return high, (x - high.astype(F32)).astype(BF16)


def dot(a, b):
    return jnp.dot(a, b, preferred_element_type=F32)


def column_hits(cell, columns):
    return jnp.where(
        lax.broadcasted_iota(jnp.int32, (columns, cell.shape[1]), 0) == cell % columns, 1.0, 0.0
    ).astype(BF16)


def adjoint(values, weights_ref, cell_ref, rows, columns):
    levels, slots = weights_ref.shape
    total = levels * rows
    chunk = 256
    field = jnp.zeros((2 * total, columns), F32)
    for start in range(0, slots, chunk):
        cell = cell_ref[:, start : start + chunk]
        hits = column_hits(cell, columns)
        here = lax.broadcasted_iota(jnp.int32, (rows, chunk), 0) == cell // columns
        weighted = weights_ref[:, start : start + chunk] * values[:, start : start + chunk]
        parts = [jnp.where(here, weighted[level : level + 1], 0.0) for level in range(levels)]
        high, low = split(jnp.concatenate(parts, axis=0))
        both = jnp.concatenate([high, low], axis=0)
        field = field + lax.dot_general(both, hits, (((1,), (1,)), ((), ())), preferred_element_type=F32)
    return field[:total] + field[total:]


def observe(field, weights_ref, cell_ref, live, rows, columns):
    levels, slots = weights_ref.shape
    chunk = 256
    high, low = split(field)
    both = jnp.concatenate([high, low], axis=1)
    observed = []
    for start in range(0, slots, chunk):
        cell = cell_ref[:, start : start + chunk]
        hits = column_hits(cell, columns)
        picked = dot(both, jnp.concatenate([hits, hits], axis=0))
        here = lax.broadcasted_iota(jnp.int32, (rows, chunk), 0) == cell // columns
        total = jnp.zeros((rows, chunk), F32)
        for level in range(levels):
            weight = weights_ref[level : level + 1, start : start + chunk]
            total = total + jnp.where(here, picked[level * rows : (level + 1) * rows], 0.0) * weight
        observed.append(jnp.sum(total, axis=0, keepdims=True))
    return jnp.concatenate(observed, axis=1) * live


def live_slots(count_ref, slots):
    return jnp.where(lax.broadcasted_iota(jnp.int32, (1, slots), 1) < count_ref[0], 1.0, 0.0)


def localized(first, p_refs, g_refs, rows_ref, pair_high_ref, pair_low_ref):
    total = g_refs[0].shape[0]
    sides = []
    for member in (first, first + 1):
        sides.append(jnp.concatenate([p[member].astype(F32) * g[...] for p, g in zip(p_refs, g_refs)], axis=0))
    high, low = split(jnp.concatenate(sides, axis=1))
    mixed = dot(rows_ref[...], high)
    mixed = mixed[:total] + mixed[total:] + dot(rows_ref[:total], low)
    high, low = split(mixed)
    across = dot(jnp.concatenate([high, low], axis=0), pair_high_ref[...])
    return across[:total] + across[total:] + dot(high, pair_low_ref[...])


def as_rows(line, width=128):
    return jnp.concatenate([line[:, i : i + width] for i in range(0, line.shape[1], width)], axis=0)


def as_line(block):
    return jnp.concatenate([block[i : i + 1] for i in range(block.shape[0])], axis=1)


def start_kernel(rows, columns, count, weights, cell, precision, innovations, field):
    live = live_slots(count, weights.shape[1])
    values = live * precision[...] * innovations[...]
    field[...] = adjoint(values, weights, cell, rows, columns)


def forward_kernel(rows, columns, count, p0, p1, p2, g0, g1, g2, mix, pair_high, pair_low, weights, cell, message):
    members = p0.shape[0]
    field = jnp.zeros(g0.shape, F32)
    for first in range(0, members, 2):
        spread = localized(first, (p0, p1, p2), (g0, g1, g2), mix, pair_high, pair_low)
        field = field + p1[first].astype(F32) * spread[:, :columns] + p1[first + 1].astype(F32) * spread[:, columns:]
    observed = as_rows(observe(field, weights, cell, live_slots(count, weights.shape[1]), rows, columns))
    peers = message.shape[0]
    lines = observed.shape[0]
    share = field.shape[0] // peers
    for peer in range(peers):
        message[peer, :lines] = observed
        message[peer, lines:] = field[peer * share : (peer + 1) * share]


def middle_kernel(rows, columns, count, message, weights, cell, precision, field, observed, share):
    summed = jnp.sum(message[...], axis=0)
    lines = observed.shape[0]
    observed[...] = summed[:lines]
    share[...] = summed[lines:]
    values = precision[...] * as_line(summed[:lines])
    field[...] = adjoint(values, weights, cell, rows, columns)


def alpha_kernel(p0, p1, p2, g0, g1, g2, mix, pair_high, pair_low, alpha):
    columns = g0.shape[1]
    for first in range(0, p0.shape[0], 2):
        spread = localized(first, (p0, p1, p2), (g0, g1, g2), mix, pair_high, pair_low)
        alpha[first] = spread[:, :columns]
        alpha[first + 1] = spread[:, columns:]


def scalars_kernel(count, message, once, precision, innovations, scalars, share):
    summed = jnp.sum(message[...], axis=0)
    lines = once.shape[0]
    share[...] = summed[lines:]
    z2 = summed[:lines]
    z1 = once[...]
    rho = precision[...]
    slot = lax.broadcasted_iota(jnp.int32, rho.shape, 0) * rho.shape[1] + lax.broadcasted_iota(jnp.int32, rho.shape, 1)
    c = jnp.where(slot < count[0], rho * innovations[...], 0.0)

    def total(x):
        return jnp.sum(jnp.sum(x, axis=0, keepdims=True), axis=1, keepdims=True)

    d = c + rho * z1
    e = z1 + z2
    size = total(d * d)
    shift = jnp.where(size > 0.0, total(c * d) / jnp.where(size > 0.0, size, 1.0), 0.0)
    v = c - shift * d
    w = z1 - shift * e
    values = [
        shift,
        total(c * z1),
        total(d * z1),
        total(v * w),
        total(v * e + d * w),
        total(d * e),
        total(v * z1 + c * w),
        total(d * z1 + c * e),
        total(rho * w * w),
        total(rho * w * e),
        total(rho * e * e),
        total(rho * w * z1),
        total(rho * e * z1),
        total(rho * z1 * z1),
    ]
    lane = lax.broadcasted_iota(jnp.int32, (1, scalars.shape[1]), 1)
    line = jnp.zeros((1, scalars.shape[1]), F32)
    for i, value in enumerate(values):
        line = jnp.where(lane == i, value, line)
    scalars[...] = jnp.broadcast_to(line, scalars.shape)


def final_kernel(scalars, alpha0, alpha1, inc0, inc1, alpha, increment):
    table = scalars[...]

    def column(i):
        return table[:, i : i + 1]

    def total(x):
        return jnp.sum(x, axis=0, keepdims=True)

    cz = total(column(1))
    step0 = cz / total(column(2))
    delta = step0 - column(0)
    rr1 = total(column(3) - delta * column(4) + delta * delta * column(5))
    beta = rr1 / cz
    pq1 = rr1 + beta * total(column(6) - delta * column(7)) + beta * beta * cz
    pq1 = pq1 + total(column(8) - 2.0 * delta * column(9) + delta * delta * column(10))
    pq1 = pq1 + 2.0 * beta * total(column(11) - delta * column(12)) + beta * beta * total(column(13))
    step1 = rr1 / pq1
    first = step0 + step1 * (1.0 - step0 + beta)
    second = -step1 * step0
    increment[...] = first * inc0[...] + second * inc1[...]
    for member in range(alpha.shape[0]):
        alpha[member] = first * alpha0[member] + second * alpha1[member]


def call(kernel, outs, *args):
    smem = [0] if args[0].dtype == jnp.int32 and args[0].shape == (1,) else []
    vmem = pl.BlockSpec(memory_space=pltpu.VMEM)
    single = not isinstance(outs, list)
    shapes = [jax.ShapeDtypeStruct(shape, F32) for shape in ([outs] if single else outs)]
    return pl.pallas_call(
        kernel,
        out_shape=shapes[0] if single else shapes,
        in_specs=[pl.BlockSpec(memory_space=pltpu.SMEM) if i in smem else vmem for i in range(len(args))],
        out_specs=vmem if single else [vmem] * len(shapes),
        compiler_params=pltpu.CompilerParams(vmem_limit_bytes=VMEM_LIMIT),
    )(*args)


def neighbours(x):
    size = lax.axis_size("tile")
    up = [(i, (i + 1) % size) for i in range(size)]
    down = [(j, i) for i, j in up]
    return lax.ppermute(x, "tile", up), lax.ppermute(x, "tile", down)


def local(perturbations, innovations, obs_precision, obs_weights, obs_cell, obs_count):
    members, levels, rows, columns = perturbations.shape
    slots = obs_cell.shape[0]
    cells = levels * rows
    ens, tiles = lax.axis_size("ens"), lax.axis_size("tile")
    everyone = ens * members
    lines = slots // 128
    share = cells // ens
    mix2, high2, low2 = local_matrices(levels, rows, columns, 2, 1.0 / everyone)
    mix1, high1, low1 = local_matrices(levels, rows, columns, 1, 1.0 / math.sqrt(everyone))

    p = perturbations.reshape(members, cells, columns)
    p_before, p_after = neighbours(p)
    cell = obs_cell.reshape(1, slots)
    precision = obs_precision.reshape(1, slots)
    innovations_line = innovations.reshape(1, slots)
    shape = (rows, columns)

    def bound(kernel):
        def run(*refs):
            kernel(*shape, *refs)

        return run

    def forward(g, g_before, g_after):
        return call(
            bound(forward_kernel), (ens, lines + share, columns),
            obs_count, p_before, p, p_after, g_before, g, g_after, mix2, high2, low2, obs_weights, cell,
        )

    def alpha_of(g, g_before, g_after):
        return call(
            alpha_kernel, (members, cells, columns),
            p_before, p, p_after, g_before, g, g_after, mix1, high1, low1,
        )

    g0 = call(bound(start_kernel), (cells, columns), obs_count, obs_weights, cell, precision, innovations_line)
    g0_before, g0_after = neighbours(g0)
    message = lax.all_to_all(forward(g0, g0_before, g0_after), "ens", 0, 0)
    g1, once, share0 = call(
        bound(middle_kernel), [(cells, columns), (lines, 128), (share, columns)],
        obs_count, message, obs_weights, cell, precision,
    )
    g1_before, g1_after = neighbours(g1)
    alpha0 = alpha_of(g0, g0_before, g0_after)
    message = lax.all_to_all(forward(g1, g1_before, g1_after), "ens", 0, 0)
    scalars, share1 = call(
        scalars_kernel, [(tiles, 128), (share, columns)],
        obs_count, message, once, obs_precision.reshape(lines, 128), innovations.reshape(lines, 128),
    )
    alpha1 = alpha_of(g1, g1_before, g1_after)
    both = jnp.concatenate([share0, share1], axis=0)
    both = lax.all_to_all(jnp.broadcast_to(both[None], (ens,) + both.shape), "ens", 0, 0)
    inc0 = both[:, :share].reshape(cells, columns)
    inc1 = both[:, share:].reshape(cells, columns)
    scalars = lax.all_to_all(scalars, "tile", 0, 0, tiled=True)
    alpha, increment = call(
        final_kernel, [(members, cells, columns), (cells, columns)],
        scalars, alpha0, alpha1, inc0, inc1,
    )
    return alpha.reshape(perturbations.shape), increment.reshape(levels, rows, columns)


def solution(mesh):
    placed = (
        P("ens", None, "tile", None),
        P("tile"),
        P("tile"),
        P(None, "tile"),
        P("tile"),
        P("tile"),
    )
    return jax.shard_map(
        local,
        mesh=mesh,
        in_specs=placed,
        out_specs=(P("ens", None, "tile", None), P(None, "tile", None)),
        check_vma=False,
    )
```

```python
import math

import jax
import jax.numpy as jnp
import numpy as np
from jax import lax
from jax.experimental import pallas as pl
from jax.experimental.pallas import tpu as pltpu
from jax.sharding import PartitionSpec as P

F32 = jnp.float32
BF16 = jnp.bfloat16
VERTICAL_SPREAD = 2.0
CORES = 2
VMEM_LIMIT = 12 * 1024 * 1024


def gauss(radius, spread):
    offsets = np.arange(-radius, radius + 1) / spread
    return np.exp(-offsets * offsets)


def band(length, spread):
    position = np.arange(length)
    spacing = (position[:, None] - position[None, :]) / spread
    return np.exp(-spacing * spacing) / np.sqrt(np.sum(gauss(length, spread) ** 2))


def bf16_pair(matrix):
    matrix = matrix.astype(np.float32)
    high = matrix.astype(jnp.bfloat16)
    low = (matrix - high.astype(np.float32)).astype(jnp.bfloat16)
    return high, low


def local_matrices(levels, rows, columns, power, scale):
    radius = rows // 2
    kernel = gauss(radius, float(radius))
    kernel = kernel / np.sqrt(np.sum(kernel * kernel))
    vertical = band(levels, VERTICAL_SPREAD)
    lateral = band(columns, columns / 16.0)
    if power == 2:
        kernel = np.convolve(kernel, kernel)
        vertical = vertical @ vertical
        lateral = lateral @ lateral
    reach = (len(kernel) - 1) // 2
    blocks = []
    for tile in (-1, 0, 1):
        offset = tile * rows + np.arange(rows)[None, :] - np.arange(rows)[:, None]
        inside = np.abs(offset) <= reach
        along = np.where(inside, kernel[np.clip(offset + reach, 0, 2 * reach)], 0.0)
        blocks.append(np.kron(vertical, along))
    rows_high, rows_low = bf16_pair(np.concatenate(blocks, axis=1) * scale)
    pair_high, pair_low = bf16_pair(np.kron(np.eye(2), lateral))
    mix = np.concatenate([rows_high, rows_low], axis=0)
    total = levels * rows
    own = mix[:, total : 2 * total]
    sides = np.concatenate([mix[:, :total], mix[:, 2 * total :]], axis=1)
    return mix, own, sides, pair_high, pair_low


def split(x):
    high = x.astype(BF16)
    return high, (x - high.astype(F32)).astype(BF16)


def dot(a, b):
    return jnp.dot(a, b, preferred_element_type=F32)


def column_hits(cell, columns):
    return jnp.where(
        lax.broadcasted_iota(jnp.int32, (columns, cell.shape[1]), 0) == cell % columns, 1.0, 0.0
    ).astype(BF16)


def adjoint(values, weights_ref, cell_ref, rows, columns):
    levels, slots = weights_ref.shape
    total = levels * rows
    chunk = 256
    field = jnp.zeros((2 * total, columns), F32)
    for start in range(0, slots, chunk):
        cell = cell_ref[:, start : start + chunk]
        hits = column_hits(cell, columns)
        here = lax.broadcasted_iota(jnp.int32, (rows, chunk), 0) == cell // columns
        weighted = weights_ref[:, start : start + chunk] * values[:, start : start + chunk]
        parts = [jnp.where(here, weighted[level : level + 1], 0.0) for level in range(levels)]
        high, low = split(jnp.concatenate(parts, axis=0))
        both = jnp.concatenate([high, low], axis=0)
        field = field + lax.dot_general(both, hits, (((1,), (1,)), ((), ())), preferred_element_type=F32)
    return field[:total] + field[total:]


def observe(field, weights_ref, cell_ref, live, rows, columns):
    levels, slots = weights_ref.shape
    chunk = 256
    high, low = split(field)
    both = jnp.concatenate([high, low], axis=1)
    observed = []
    for start in range(0, slots, chunk):
        cell = cell_ref[:, start : start + chunk]
        hits = column_hits(cell, columns)
        picked = dot(both, jnp.concatenate([hits, hits], axis=0))
        here = lax.broadcasted_iota(jnp.int32, (rows, chunk), 0) == cell // columns
        total = jnp.zeros((rows, chunk), F32)
        for level in range(levels):
            weight = weights_ref[level : level + 1, start : start + chunk]
            total = total + jnp.where(here, picked[level * rows : (level + 1) * rows], 0.0) * weight
        observed.append(jnp.sum(total, axis=0, keepdims=True))
    return jnp.concatenate(observed, axis=1) * live


def live_slots(count_ref, slots):
    return jnp.where(lax.broadcasted_iota(jnp.int32, (1, slots), 1) < count_ref[0], 1.0, 0.0)


def localized(first, p_refs, g_refs, rows_ref, pair_high_ref, pair_low_ref):
    total = g_refs[0].shape[0]
    sides = []
    for member in (first, first + 1):
        sides.append(jnp.concatenate([p[member].astype(F32) * g[...] for p, g in zip(p_refs, g_refs)], axis=0))
    high, low = split(jnp.concatenate(sides, axis=1))
    mixed = dot(rows_ref[...], high)
    mixed = mixed[:total] + mixed[total:] + dot(rows_ref[:total], low)
    high, low = split(mixed)
    across = dot(jnp.concatenate([high, low], axis=0), pair_high_ref[...])
    return across[:total] + across[total:] + dot(high, pair_low_ref[...])


def summed_members(field, weigh, p_refs, g_refs, rows_ref, pair_high_ref, pair_low_ref):
    columns = g_refs[0].shape[1]
    for first in range(0, weigh.shape[0], 2):
        spread = localized(first, p_refs, g_refs, rows_ref, pair_high_ref, pair_low_ref)
        field = field + weigh[first].astype(F32) * spread[:, :columns]
        field = field + weigh[first + 1].astype(F32) * spread[:, columns:]
    return field


def as_rows(line, width=128):
    return jnp.concatenate([line[:, i : i + width] for i in range(0, line.shape[1], width)], axis=0)


def as_line(block):
    return jnp.concatenate([block[i : i + 1] for i in range(block.shape[0])], axis=1)


def start_kernel(rows, columns, count, weights, cell, precision, innovations, field):
    live = live_slots(count, weights.shape[1])
    values = live * precision[...] * innovations[...]
    field[...] = adjoint(values, weights, cell, rows, columns)


def own_kernel(p, g, mix, pair_high, pair_low, field):
    field[...] = summed_members(jnp.zeros(g.shape, F32), p, [p], [g], mix, pair_high, pair_low)


def forward_kernel(rows, columns, count, place, p0, p, p2, g0, g2, own, mix, pair_high, pair_low, weights, cell, kept, given, whole):
    field = summed_members(own[...], p, [p0, p2], [g0, g2], mix, pair_high, pair_low)
    whole[...] = field
    observed = as_rows(observe(field, weights, cell, live_slots(count, weights.shape[1]), rows, columns))
    lines = observed.shape[0]
    half = field.shape[0] // CORES
    core = lax.rem(place[0], CORES)
    for message, at in ((kept, core), (given, 1 - core)):
        message[:lines] = observed
        message[lines:] = whole[pl.ds(pl.multiple_of(at * half, half), half)]


def middle_kernel(rows, columns, count, *refs):
    *messages, weights, cell, precision, after, field, observed = refs
    summed = sum(message[...] for message in messages)
    observed[...] = summed
    field[...] = adjoint(precision[...] * as_line(summed), weights, cell, rows, columns)


def alpha_kernel(p0, p1, p2, g0, g1, g2, mix, pair_high, pair_low, after, alpha):
    columns = g0.shape[1]
    for first in range(0, p0.shape[0], 2):
        spread = localized(first, (p0, p1, p2), (g0, g1, g2), mix, pair_high, pair_low)
        alpha[first] = spread[:, :columns]
        alpha[first + 1] = spread[:, columns:]


def scalars_kernel(count, *refs):
    *messages, once, precision, innovations, after, scalars, half = refs
    lines = once.shape[0]
    z2 = sum(message[:lines] for message in messages)
    half[...] = sum(message[lines:] for message in messages)
    z1 = once[...]
    rho = precision[...]
    slot = lax.broadcasted_iota(jnp.int32, rho.shape, 0) * rho.shape[1] + lax.broadcasted_iota(jnp.int32, rho.shape, 1)
    c = jnp.where(slot < count[0], rho * innovations[...], 0.0)

    def total(x):
        return jnp.sum(jnp.sum(x, axis=0, keepdims=True), axis=1, keepdims=True)

    d = c + rho * z1
    e = z1 + z2
    size = total(d * d)
    shift = jnp.where(size > 0.0, total(c * d) / jnp.where(size > 0.0, size, 1.0), 0.0)
    v = c - shift * d
    w = z1 - shift * e
    values = [
        shift,
        total(c * z1),
        total(d * z1),
        total(v * w),
        total(v * e + d * w),
        total(d * e),
        total(v * z1 + c * w),
        total(d * z1 + c * e),
        total(rho * w * w),
        total(rho * w * e),
        total(rho * e * e),
        total(rho * w * z1),
        total(rho * e * z1),
        total(rho * z1 * z1),
    ]
    lane = lax.broadcasted_iota(jnp.int32, (1, scalars.shape[1]), 1)
    line = jnp.zeros((1, scalars.shape[1]), F32)
    for i, value in enumerate(values):
        line = jnp.where(lane == i, value, line)
    scalars[...] = jnp.broadcast_to(line, scalars.shape)


def combination(scalars):
    table = scalars[...]

    def column(i):
        return table[:, i : i + 1]

    def total(x):
        return jnp.sum(x, axis=0, keepdims=True)

    cz = total(column(1))
    step0 = cz / total(column(2))
    delta = step0 - column(0)
    rr1 = total(column(3) - delta * column(4) + delta * delta * column(5))
    beta = rr1 / cz
    pq1 = rr1 + beta * total(column(6) - delta * column(7)) + beta * beta * cz
    pq1 = pq1 + total(column(8) - 2.0 * delta * column(9) + delta * delta * column(10))
    pq1 = pq1 + 2.0 * beta * total(column(11) - delta * column(12)) + beta * beta * total(column(13))
    step1 = rr1 / pq1
    return step0 + step1 * (1.0 - step0 + beta), -step1 * step0


def final_kernel(scalars, alpha0, alpha1, alpha):
    first, second = combination(scalars)
    for member in range(alpha.shape[0]):
        alpha[member] = first * alpha0[member] + second * alpha1[member]


def increment_kernel(place, scalars, mine0, mine1, other0, other1, increment):
    first, second = combination(scalars)
    core = lax.rem(place[0], CORES)
    half = mine0.shape[0]
    for part0, part1, at in ((mine0, mine1, core), (other0, other1, 1 - core)):
        increment[pl.ds(pl.multiple_of(at * half, half), half)] = first * part0[...] + second * part1[...]


def in_vmem(x):
    return x, pl.BlockSpec(memory_space=pltpu.VMEM)


def in_smem(x):
    return x, pl.BlockSpec(memory_space=pltpu.SMEM)


def anywhere(x):
    return x, pl.BlockSpec(memory_space=pl.ANY)


def call(kernel, outs, args, scratch=()):
    single = not isinstance(outs, list)
    shapes = [jax.ShapeDtypeStruct(shape, F32) for shape in ([outs] if single else outs)]
    out_spec = pl.BlockSpec(memory_space=pltpu.VMEM)
    return pl.pallas_call(
        kernel,
        out_shape=shapes[0] if single else shapes,
        in_specs=[spec for _, spec in args],
        out_specs=out_spec if single else [out_spec] * len(shapes),
        scratch_shapes=list(scratch),
        compiler_params=pltpu.CompilerParams(vmem_limit_bytes=VMEM_LIMIT),
    )(*[x for x, _ in args])


def neighbours(x):
    size = lax.axis_size("tile")
    up = [(i, (i + 1) % size) for i in range(size)]
    down = [(j, i) for i, j in up]
    return lax.ppermute(x, "tile", up), lax.ppermute(x, "tile", down)


def local(perturbations, innovations, obs_precision, obs_weights, obs_cell, obs_count):
    members, levels, rows, columns = perturbations.shape
    slots = obs_cell.shape[0]
    cells = levels * rows
    ens, tiles = lax.axis_size("ens"), lax.axis_size("tile")
    everyone = ens * members
    lines = slots // 128
    _, own2, sides2, high2, low2 = local_matrices(levels, rows, columns, 2, 1.0 / everyone)
    mix1, _, _, high1, low1 = local_matrices(levels, rows, columns, 1, 1.0 / math.sqrt(everyone))

    p = perturbations.reshape(members, cells, columns)
    p_before, p_after = neighbours(p)
    cell = obs_cell.reshape(1, slots)
    precision = obs_precision.reshape(1, slots)
    innovations_line = innovations.reshape(1, slots)
    shape = (rows, columns)

    def bound(kernel):
        def run(*refs):
            kernel(*shape, *refs)

        return run

    field_shape = (cells, columns)
    half = cells // CORES
    chips = ens // CORES
    place = lax.axis_index("ens").reshape(1)
    vmem = lambda *xs: [in_vmem(x) for x in xs]

    def own(g):
        return call(own_kernel, field_shape, vmem(p, g, own2, high2, low2))

    def forward(own_part, g_before, g_after):
        kept, given = call(
            bound(forward_kernel), [(lines + half, columns)] * 2,
            [in_smem(obs_count), in_smem(place)]
            + vmem(p_before, p, p_after, g_before, g_after, own_part, sides2, high2, low2, obs_weights, cell),
            [pltpu.VMEM(field_shape, F32)],
        )
        return kept + other_core(given)

    def other_core(x):
        return lax.ppermute(x, "ens", [(i, i ^ 1) for i in range(ens)])

    def from_chips(x):
        arrived = [x]
        for back in range(1, chips):
            route = [(c * CORES + core, (c + back) % chips * CORES + core) for c in range(chips) for core in range(CORES)]
            arrived.append(lax.ppermute(x, "ens", route))
        return arrived

    def alpha_of(g, g_before, g_after, after):
        return call(
            alpha_kernel, (members, cells, columns),
            vmem(p_before, p, p_after, g_before, g, g_after, mix1, high1, low1) + [anywhere(after)],
        )

    g0 = call(
        bound(start_kernel), field_shape,
        [in_smem(obs_count)] + vmem(obs_weights, cell, precision, innovations_line),
    )
    g0_before, g0_after = neighbours(g0)
    sent = forward(own(g0), g0_before, g0_after)
    messages = from_chips(sent[:lines])
    alpha0 = alpha_of(g0, g0_before, g0_after, sent)
    g1, once = call(
        bound(middle_kernel), [field_shape, (lines, 128)],
        [in_smem(obs_count)] + vmem(*messages, obs_weights, cell, precision) + [anywhere(alpha0)],
    )
    g1_before, g1_after = neighbours(g1)
    own_part = own(g1)
    half0, own_part = lax.optimization_barrier((sent[lines:], own_part))
    half0 = sum(from_chips(half0))
    sent = forward(own_part, g1_before, g1_after)
    messages = from_chips(sent)
    alpha1 = alpha_of(g1, g1_before, g1_after, sent)
    scalars, half1 = call(
        scalars_kernel, [(tiles, 128), (half, columns)],
        [in_smem(obs_count)] + vmem(*messages, once, obs_precision.reshape(lines, 128), innovations.reshape(lines, 128))
        + [anywhere(alpha1)],
    )
    other0, other1 = other_core(half0), other_core(half1)
    scalars = lax.all_to_all(scalars.reshape(tiles, 1, 128), "tile", 0, 0).reshape(tiles, 128)
    alpha = call(final_kernel, (members, cells, columns), vmem(scalars, alpha0, alpha1))
    increment = call(
        increment_kernel, field_shape, [in_smem(place)] + vmem(scalars, half0, half1, other0, other1)
    )
    return alpha.reshape(perturbations.shape), increment.reshape(levels, rows, columns)


def solution(mesh):
    placed = (
        P("ens", None, "tile", None),
        P("tile"),
        P("tile"),
        P(None, "tile"),
        P("tile"),
        P("tile"),
    )
    return jax.shard_map(
        local,
        mesh=mesh,
        in_specs=placed,
        out_specs=(P("ens", None, "tile", None), P(None, "tile", None)),
        check_vma=False,
    )
```

```python
import math

import jax
import jax.numpy as jnp
import numpy as np
from jax import lax
from jax.experimental import pallas as pl
from jax.experimental.pallas import tpu as pltpu
from jax.sharding import PartitionSpec as P

F32 = jnp.float32
BF16 = jnp.bfloat16
VERTICAL_SPREAD = 2.0
CORES = 2
VMEM_LIMIT = 12 * 1024 * 1024


def gauss(radius, spread):
    offsets = np.arange(-radius, radius + 1) / spread
    return np.exp(-offsets * offsets)


def band(length, spread):
    position = np.arange(length)
    spacing = (position[:, None] - position[None, :]) / spread
    return np.exp(-spacing * spacing) / np.sqrt(np.sum(gauss(length, spread) ** 2))


def bf16_pair(matrix):
    matrix = matrix.astype(np.float32)
    high = matrix.astype(jnp.bfloat16)
    low = (matrix - high.astype(np.float32)).astype(jnp.bfloat16)
    return high, low


def local_matrices(levels, rows, columns, power, scale):
    radius = rows // 2
    kernel = gauss(radius, float(radius))
    kernel = kernel / np.sqrt(np.sum(kernel * kernel))
    vertical = band(levels, VERTICAL_SPREAD)
    lateral = band(columns, columns / 16.0)
    if power == 2:
        kernel = np.convolve(kernel, kernel)
        vertical = vertical @ vertical
        lateral = lateral @ lateral
    reach = (len(kernel) - 1) // 2
    blocks = []
    for tile in (-1, 0, 1):
        offset = tile * rows + np.arange(rows)[None, :] - np.arange(rows)[:, None]
        inside = np.abs(offset) <= reach
        along = np.where(inside, kernel[np.clip(offset + reach, 0, 2 * reach)], 0.0)
        blocks.append(np.kron(vertical, along))
    rows_high, rows_low = bf16_pair(np.concatenate(blocks, axis=1) * scale)
    pair_high, pair_low = bf16_pair(np.kron(np.eye(2), lateral))
    mix = np.concatenate([rows_high, rows_low], axis=0)
    total = levels * rows
    return mix, [mix[:, i : i + total] for i in range(0, 3 * total, total)], pair_high, pair_low


def split(x):
    high = x.astype(BF16)
    return high, (x - high.astype(F32)).astype(BF16)


def dot(a, b):
    return jnp.dot(a, b, preferred_element_type=F32)


def column_hits(cell, columns):
    return jnp.where(
        lax.broadcasted_iota(jnp.int32, (columns, cell.shape[1]), 0) == cell % columns, 1.0, 0.0
    ).astype(BF16)


def adjoint(values, weights_ref, cell_ref, rows, columns):
    levels, slots = weights_ref.shape
    total = levels * rows
    chunk = 256
    field = jnp.zeros((2 * total, columns), F32)
    for start in range(0, slots, chunk):
        cell = cell_ref[:, start : start + chunk]
        hits = column_hits(cell, columns)
        here = lax.broadcasted_iota(jnp.int32, (rows, chunk), 0) == cell // columns
        weighted = weights_ref[:, start : start + chunk] * values[:, start : start + chunk]
        parts = [jnp.where(here, weighted[level : level + 1], 0.0) for level in range(levels)]
        high, low = split(jnp.concatenate(parts, axis=0))
        both = jnp.concatenate([high, low], axis=0)
        field = field + lax.dot_general(both, hits, (((1,), (1,)), ((), ())), preferred_element_type=F32)
    return field[:total] + field[total:]


def observe(field, weights_ref, cell_ref, live, rows, columns):
    levels, slots = weights_ref.shape
    chunk = 256
    high, low = split(field)
    both = jnp.concatenate([high, low], axis=1)
    observed = []
    for start in range(0, slots, chunk):
        cell = cell_ref[:, start : start + chunk]
        hits = column_hits(cell, columns)
        picked = dot(both, jnp.concatenate([hits, hits], axis=0))
        here = lax.broadcasted_iota(jnp.int32, (rows, chunk), 0) == cell // columns
        total = jnp.zeros((rows, chunk), F32)
        for level in range(levels):
            weight = weights_ref[level : level + 1, start : start + chunk]
            total = total + jnp.where(here, picked[level * rows : (level + 1) * rows], 0.0) * weight
        observed.append(jnp.sum(total, axis=0, keepdims=True))
    return jnp.concatenate(observed, axis=1) * live


def live_slots(count_ref, slots):
    return jnp.where(lax.broadcasted_iota(jnp.int32, (1, slots), 1) < count_ref[0], 1.0, 0.0)


def mixed_pairs(p_refs, g_refs, rows_ref, mixed):
    total = g_refs[0].shape[0]
    for pair in range(mixed.shape[0]):
        sides = []
        for member in (2 * pair, 2 * pair + 1):
            sides.append(jnp.concatenate([p[member].astype(F32) * g[...] for p, g in zip(p_refs, g_refs)], axis=0))
        high, low = split(jnp.concatenate(sides, axis=1))
        product = dot(rows_ref[...], high)
        high, low = split(product[:total] + product[total:] + dot(rows_ref[:total], low))
        mixed[pair, :total] = high
        mixed[pair, total:] = low


def across_columns(pair, mixed, pair_high_ref, pair_low_ref):
    total = mixed.shape[1] // 2
    product = dot(mixed[pair], pair_high_ref[...])
    return product[:total] + product[total:] + dot(mixed[pair, :total], pair_low_ref[...])


def summed_members(field, weigh, p_refs, g_refs, rows_ref, pair_high_ref, pair_low_ref, mixed):
    columns = g_refs[0].shape[1]
    mixed_pairs(p_refs, g_refs, rows_ref, mixed)
    for pair in range(mixed.shape[0]):
        spread = across_columns(pair, mixed, pair_high_ref, pair_low_ref)
        field = field + weigh[2 * pair].astype(F32) * spread[:, :columns]
        field = field + weigh[2 * pair + 1].astype(F32) * spread[:, columns:]
    return field


def as_rows(line, width=128):
    return jnp.concatenate([line[:, i : i + width] for i in range(0, line.shape[1], width)], axis=0)


def as_line(block):
    return jnp.concatenate([block[i : i + 1] for i in range(block.shape[0])], axis=1)


def start_kernel(rows, columns, count, weights, cell, precision, innovations, field):
    live = live_slots(count, weights.shape[1])
    values = live * precision[...] * innovations[...]
    field[...] = adjoint(values, weights, cell, rows, columns)


def own_kernel(p, g, mix, pair_high, pair_low, field, mixed):
    field[...] = summed_members(jnp.zeros(g.shape, F32), p, [p], [g], mix, pair_high, pair_low, mixed)


def side_kernel(p, p_side, g_side, part, mix, pair_high, pair_low, field, mixed):
    field[...] = summed_members(part[...], p, [p_side], [g_side], mix, pair_high, pair_low, mixed)


def first_kernel(rows, columns, count, p, p_side, g_side, part, mix, pair_high, pair_low, weights, cell, observed, field, mixed):
    whole = summed_members(part[...], p, [p_side], [g_side], mix, pair_high, pair_low, mixed)
    observed[...] = as_rows(observe(whole, weights, cell, live_slots(count, weights.shape[1]), rows, columns))
    field[...] = whole


def second_kernel(rows, columns, count, place, p, p_side, g_side, part, mix, pair_high, pair_low, weights, cell, field0,
                  kept, given, field1, mixed):
    whole = summed_members(part[...], p, [p_side], [g_side], mix, pair_high, pair_low, mixed)
    field1[...] = whole
    observed = as_rows(observe(whole, weights, cell, live_slots(count, weights.shape[1]), rows, columns))
    lines = observed.shape[0]
    half = whole.shape[0] // CORES
    core = lax.rem(place[0], CORES)
    for message, at in ((kept, core), (given, 1 - core)):
        rows_of_half = pl.ds(pl.multiple_of(at * half, half), half)
        message[:lines] = observed
        message[lines : lines + half] = field0[rows_of_half]
        message[lines + half :] = field1[rows_of_half]


def middle_kernel(rows, columns, count, *refs):
    *messages, weights, cell, precision, after, field, observed = refs
    summed = sum(message[...] for message in messages)
    observed[...] = summed
    field[...] = adjoint(precision[...] * as_line(summed), weights, cell, rows, columns)


def alpha_kernel(p0, p1, p2, g0, g1, g2, mix, pair_high, pair_low, after, alpha, mixed):
    columns = g0.shape[1]
    mixed_pairs((p0, p1, p2), (g0, g1, g2), mix, mixed)
    for pair in range(mixed.shape[0]):
        spread = across_columns(pair, mixed, pair_high, pair_low)
        alpha[2 * pair] = spread[:, :columns]
        alpha[2 * pair + 1] = spread[:, columns:]


def scalars_kernel(count, *refs):
    *messages, once, precision, innovations, after, scalars, halves = refs
    lines = once.shape[0]
    z2 = sum(message[:lines] for message in messages)
    half = halves.shape[1]
    for i in range(2):
        halves[i] = sum(message[lines + i * half : lines + (i + 1) * half] for message in messages)
    z1 = once[...]
    rho = precision[...]
    slot = lax.broadcasted_iota(jnp.int32, rho.shape, 0) * rho.shape[1] + lax.broadcasted_iota(jnp.int32, rho.shape, 1)
    c = jnp.where(slot < count[0], rho * innovations[...], 0.0)

    def total(x):
        return jnp.sum(jnp.sum(x, axis=0, keepdims=True), axis=1, keepdims=True)

    d = c + rho * z1
    e = z1 + z2
    size = total(d * d)
    shift = jnp.where(size > 0.0, total(c * d) / jnp.where(size > 0.0, size, 1.0), 0.0)
    v = c - shift * d
    w = z1 - shift * e
    values = [
        shift,
        total(c * z1),
        total(d * z1),
        total(v * w),
        total(v * e + d * w),
        total(d * e),
        total(v * z1 + c * w),
        total(d * z1 + c * e),
        total(rho * w * w),
        total(rho * w * e),
        total(rho * e * e),
        total(rho * w * z1),
        total(rho * e * z1),
        total(rho * z1 * z1),
    ]
    lane = lax.broadcasted_iota(jnp.int32, (1, scalars.shape[1]), 1)
    line = jnp.zeros((1, scalars.shape[1]), F32)
    for i, value in enumerate(values):
        line = jnp.where(lane == i, value, line)
    scalars[...] = jnp.broadcast_to(line, scalars.shape)


def combination(scalars):
    table = scalars[...]

    def column(i):
        return table[:, i : i + 1]

    def total(x):
        return jnp.sum(x, axis=0, keepdims=True)

    cz = total(column(1))
    step0 = cz / total(column(2))
    delta = step0 - column(0)
    rr1 = total(column(3) - delta * column(4) + delta * delta * column(5))
    beta = rr1 / cz
    pq1 = rr1 + beta * total(column(6) - delta * column(7)) + beta * beta * cz
    pq1 = pq1 + total(column(8) - 2.0 * delta * column(9) + delta * delta * column(10))
    pq1 = pq1 + 2.0 * beta * total(column(11) - delta * column(12)) + beta * beta * total(column(13))
    step1 = rr1 / pq1
    return step0 + step1 * (1.0 - step0 + beta), -step1 * step0


def final_kernel(place, scalars, alpha0, alpha1, mine, other, alpha, increment):
    first, second = combination(scalars)
    for member in range(alpha.shape[0]):
        alpha[member] = first * alpha0[member] + second * alpha1[member]
    core = lax.rem(place[0], CORES)
    half = mine.shape[1]
    for part, at in ((mine, core), (other, 1 - core)):
        increment[pl.ds(pl.multiple_of(at * half, half), half)] = first * part[0] + second * part[1]


def in_vmem(x):
    return x, pl.BlockSpec(memory_space=pltpu.VMEM)


def in_smem(x):
    return x, pl.BlockSpec(memory_space=pltpu.SMEM)


def anywhere(x):
    return x, pl.BlockSpec(memory_space=pl.ANY)


def call(kernel, outs, args, scratch=()):
    single = not isinstance(outs, list)
    shapes = [jax.ShapeDtypeStruct(shape, F32) for shape in ([outs] if single else outs)]
    out_spec = pl.BlockSpec(memory_space=pltpu.VMEM)
    return pl.pallas_call(
        kernel,
        out_shape=shapes[0] if single else shapes,
        in_specs=[spec for _, spec in args],
        out_specs=out_spec if single else [out_spec] * len(shapes),
        scratch_shapes=list(scratch),
        compiler_params=pltpu.CompilerParams(vmem_limit_bytes=VMEM_LIMIT),
    )(*[x for x, _ in args])


def neighbours(x):
    size = lax.axis_size("tile")
    up = [(i, (i + 1) % size) for i in range(size)]
    down = [(j, i) for i, j in up]
    return lax.ppermute(x, "tile", up), lax.ppermute(x, "tile", down)


def local(perturbations, innovations, obs_precision, obs_weights, obs_cell, obs_count):
    members, levels, rows, columns = perturbations.shape
    slots = obs_cell.shape[0]
    cells = levels * rows
    ens, tiles = lax.axis_size("ens"), lax.axis_size("tile")
    everyone = ens * members
    lines = slots // 128
    _, mix2, high2, low2 = local_matrices(levels, rows, columns, 2, 1.0 / everyone)
    mix1, _, high1, low1 = local_matrices(levels, rows, columns, 1, 1.0 / math.sqrt(everyone))

    p = perturbations.reshape(members, cells, columns)
    cell = obs_cell.reshape(1, slots)
    precision = obs_precision.reshape(1, slots)
    innovations_line = innovations.reshape(1, slots)
    shape = (rows, columns)

    def bound(kernel):
        def run(*refs):
            kernel(*shape, *refs)

        return run

    field_shape = (cells, columns)
    half = cells // CORES
    chips = ens // CORES
    place = lax.axis_index("ens").reshape(1)
    vmem = lambda *xs: [in_vmem(x) for x in xs]

    mixed = pltpu.VMEM((members // 2, 2 * cells, CORES * columns), BF16)

    def own_and_after(g, g_after):
        part = call(own_kernel, field_shape, vmem(p, g, mix2[1], high2, low2), [mixed])
        return call(side_kernel, field_shape, vmem(p, p_after, g_after, part, mix2[2], high2, low2), [mixed])

    def other_core(x):
        return lax.ppermute(x, "ens", [(i, i ^ 1) for i in range(ens)])

    def from_chips(x):
        arrived = [x]
        for back in range(1, chips):
            route = [(c * CORES + core, (c + back) % chips * CORES + core) for c in range(chips) for core in range(CORES)]
            arrived.append(lax.ppermute(x, "ens", route))
        return arrived

    def alpha_of(g, g_before, g_after, after):
        return call(
            alpha_kernel, (members, cells, columns),
            vmem(p_before, p, p_after, g_before, g, g_after, mix1, high1, low1) + [anywhere(after)], [mixed],
        )

    p_before, p_after = neighbours(p)
    g0 = call(
        bound(start_kernel), field_shape,
        [in_smem(obs_count)] + vmem(obs_weights, cell, precision, innovations_line),
    )
    g0_before, g0_after = neighbours(g0)
    part = own_and_after(g0, g0_after)
    seen, field0 = call(
        bound(first_kernel), [(lines, columns), field_shape],
        [in_smem(obs_count)] + vmem(p, p_before, g0_before, part, mix2[0], high2, low2, obs_weights, cell), [mixed],
    )
    sent = seen + other_core(seen)
    messages = from_chips(sent)
    alpha0 = alpha_of(g0, g0_before, g0_after, sent)
    g1, once = call(
        bound(middle_kernel), [field_shape, (lines, 128)],
        [in_smem(obs_count)] + vmem(*messages, obs_weights, cell, precision) + [anywhere(alpha0)],
    )
    g1_before, g1_after = neighbours(g1)
    part = own_and_after(g1, g1_after)
    message = (lines + 2 * half, columns)
    kept, given = call(
        bound(second_kernel), [message, message],
        [in_smem(obs_count), in_smem(place)]
        + vmem(p, p_before, g1_before, part, mix2[0], high2, low2, obs_weights, cell, field0),
        [pltpu.VMEM(field_shape, F32), mixed],
    )
    sent = kept + other_core(given)
    messages = from_chips(sent)
    alpha1 = alpha_of(g1, g1_before, g1_after, sent)
    scalars, mine = call(
        scalars_kernel, [(tiles, 128), (2, half, columns)],
        [in_smem(obs_count)]
        + vmem(*messages, once, obs_precision.reshape(lines, 128), innovations.reshape(lines, 128))
        + [anywhere(alpha1)],
    )
    other = other_core(mine)
    scalars = lax.all_to_all(scalars.reshape(tiles, 1, 128), "tile", 0, 0).reshape(tiles, 128)
    alpha, increment = call(
        final_kernel, [(members, cells, columns), field_shape],
        [in_smem(place)] + vmem(scalars, alpha0, alpha1, mine, other),
    )
    return alpha.reshape(perturbations.shape), increment.reshape(levels, rows, columns)


def solution(mesh):
    placed = (
        P("ens", None, "tile", None),
        P("tile"),
        P("tile"),
        P(None, "tile"),
        P("tile"),
        P("tile"),
    )
    return jax.shard_map(
        local,
        mesh=mesh,
        in_specs=placed,
        out_specs=(P("ens", None, "tile", None), P(None, "tile", None)),
        check_vma=False,
    )
```

```python
import math

import jax
import jax.numpy as jnp
import numpy as np
from jax import lax
from jax.experimental import pallas as pl
from jax.experimental.pallas import tpu as pltpu
from jax.sharding import PartitionSpec as P

F32 = jnp.float32
BF16 = jnp.bfloat16
VERTICAL_SPREAD = 2.0
CORES = 2
VMEM_LIMIT = 12 * 1024 * 1024


def gauss(radius, spread):
    offsets = np.arange(-radius, radius + 1) / spread
    return np.exp(-offsets * offsets)


def band(length, spread):
    position = np.arange(length)
    spacing = (position[:, None] - position[None, :]) / spread
    return np.exp(-spacing * spacing) / np.sqrt(np.sum(gauss(length, spread) ** 2))


def bf16_pair(matrix):
    matrix = matrix.astype(np.float32)
    high = matrix.astype(jnp.bfloat16)
    low = (matrix - high.astype(np.float32)).astype(jnp.bfloat16)
    return high, low


def local_matrices(levels, rows, columns, power, scale):
    radius = rows // 2
    kernel = gauss(radius, float(radius))
    kernel = kernel / np.sqrt(np.sum(kernel * kernel))
    vertical = band(levels, VERTICAL_SPREAD)
    lateral = band(columns, columns / 16.0)
    if power == 2:
        kernel = np.convolve(kernel, kernel)
        vertical = vertical @ vertical
        lateral = lateral @ lateral
    reach = (len(kernel) - 1) // 2
    blocks = []
    for tile in (-1, 0, 1):
        offset = tile * rows + np.arange(rows)[None, :] - np.arange(rows)[:, None]
        inside = np.abs(offset) <= reach
        along = np.where(inside, kernel[np.clip(offset + reach, 0, 2 * reach)], 0.0)
        blocks.append(np.concatenate(bf16_pair(np.kron(vertical, along) * scale)))
    return blocks, bf16_pair(np.kron(np.eye(CORES), lateral))


class Constants:
    def __init__(self, levels, rows, columns, members):
        self.places, arrays, start = {}, [], 0
        for power in (2, 1):
            blocks, pair = local_matrices(levels, rows, columns, power, float(members) ** (-power / 2))
            for name, array in list(zip("boa", blocks)) + list(zip("hl", pair)):
                self.places[power, name] = slice(start, start + array.shape[0])
                arrays.append(array)
                start += array.shape[0]
        self.array = np.concatenate(arrays)


def split(x):
    high = x.astype(BF16)
    return high, (x - high.astype(F32)).astype(BF16)


def dot(a, b):
    return jnp.dot(a, b, preferred_element_type=F32)


def column_hits(cell, columns):
    return jnp.where(
        lax.broadcasted_iota(jnp.int32, (columns, cell.shape[1]), 0) == cell % columns, 1.0, 0.0
    ).astype(BF16)


def adjoint(values, weights_ref, cell_ref, rows, columns):
    levels, slots = weights_ref.shape
    total = levels * rows
    chunk = 256
    field = jnp.zeros((2 * total, columns), F32)
    for start in range(0, slots, chunk):
        cell = cell_ref[:, start : start + chunk]
        hits = column_hits(cell, columns)
        here = lax.broadcasted_iota(jnp.int32, (rows, chunk), 0) == cell // columns
        weighted = weights_ref[:, start : start + chunk] * values[:, start : start + chunk]
        parts = [jnp.where(here, weighted[level : level + 1], 0.0) for level in range(levels)]
        high, low = split(jnp.concatenate(parts, axis=0))
        both = jnp.concatenate([high, low], axis=0)
        field = field + lax.dot_general(both, hits, (((1,), (1,)), ((), ())), preferred_element_type=F32)
    return field[:total] + field[total:]


def observe(field, weights_ref, cell_ref, live, rows, columns):
    levels, slots = weights_ref.shape
    chunk = 256
    high, low = split(field)
    both = jnp.concatenate([high, low], axis=1)
    observed = []
    for start in range(0, slots, chunk):
        cell = cell_ref[:, start : start + chunk]
        hits = column_hits(cell, columns)
        picked = dot(both, jnp.concatenate([hits, hits], axis=0))
        here = lax.broadcasted_iota(jnp.int32, (rows, chunk), 0) == cell // columns
        total = jnp.zeros((rows, chunk), F32)
        for level in range(levels):
            weight = weights_ref[level : level + 1, start : start + chunk]
            total = total + jnp.where(here, picked[level * rows : (level + 1) * rows], 0.0) * weight
        observed.append(jnp.sum(total, axis=0, keepdims=True))
    return jnp.concatenate(observed, axis=1) * live


def live_slots(count_ref, slots):
    return jnp.where(lax.broadcasted_iota(jnp.int32, (1, slots), 1) < count_ref[0], 1.0, 0.0)


def mixed_pairs(p_refs, g_refs, rows_matrix, mixed):
    total = g_refs[0].shape[0]
    for pair in range(mixed.shape[0]):
        sides = []
        for member in (2 * pair, 2 * pair + 1):
            sides.append(jnp.concatenate([p[member].astype(F32) * g[...] for p, g in zip(p_refs, g_refs)], axis=0))
        high, low = split(jnp.concatenate(sides, axis=1))
        product = dot(rows_matrix, high)
        high, low = split(product[:total] + product[total:] + dot(rows_matrix[:total], low))
        mixed[pair, :total] = high
        mixed[pair, total:] = low


def across_columns(pair, mixed, pair_high, pair_low):
    total = mixed.shape[1] // 2
    product = dot(mixed[pair], pair_high)
    return product[:total] + product[total:] + dot(mixed[pair, :total], pair_low)


def summed_members(field, weigh, p_side, g_side, constants, places, which, mixed):
    columns = g_side.shape[1]
    mixed_pairs([p_side], [g_side], constants[places[2, which]], mixed)
    for pair in range(mixed.shape[0]):
        spread = across_columns(pair, mixed, constants[places[2, "h"]], constants[places[2, "l"]])
        field = field + weigh[2 * pair].astype(F32) * spread[:, :columns]
        field = field + weigh[2 * pair + 1].astype(F32) * spread[:, columns:]
    return field


def as_rows(line, width=128):
    return jnp.concatenate([line[:, i : i + width] for i in range(0, line.shape[1], width)], axis=0)


def as_line(block):
    return jnp.concatenate([block[i : i + 1] for i in range(block.shape[0])], axis=1)


def start_kernel(rows, columns, count, place, weights, cell, precision, innovations, field, precision_rows, c_rows):
    c = live_slots(count, weights.shape[1]) * precision[...] * innovations[...]
    field[...] = adjoint(c, weights, cell, rows, columns)
    precision_rows[...] = as_rows(precision[...])
    c_rows[...] = as_rows(c)


def own_kernel(places, p, g, constants, field, mixed):
    field[...] = summed_members(jnp.zeros(g.shape, F32), p, p, g, constants, places, "o", mixed)


def side_kernel(places, p, p_side, g_side, part, constants, field, mixed):
    field[...] = summed_members(part[...], p, p_side, g_side, constants, places, "a", mixed)


def message_rows(place, observed, field, kept, given):
    lines = observed.shape[0]
    half = field.shape[0] // CORES
    core = lax.rem(place[0], CORES)
    for message, at in ((kept, core), (given, 1 - core)):
        message[:lines] = observed
        message[lines:] = field[pl.ds(pl.multiple_of(at * half, half), half)]


def observe_kernel(rows, columns, places, count, place, p, p_side, g_side, part, constants, weights, cell, kept, given, field, mixed):
    field[...] = summed_members(part[...], p, p_side, g_side, constants, places, "b", mixed)
    observed = as_rows(observe(field[...], weights, cell, live_slots(count, weights.shape[1]), rows, columns))
    message_rows(place, observed, field, kept, given)


def sum_kernel(first, second, total):
    total[...] = first[...] + second[...]


def middle_kernel(rows, columns, count, *refs):
    *messages, weights, cell, precision, after, field, observed, half = refs
    lines = observed.shape[0]
    half[...] = sum(message[lines:] for message in messages)
    summed = sum(message[:lines] for message in messages)
    observed[...] = summed
    field[...] = adjoint(precision[...] * as_line(summed), weights, cell, rows, columns)


def alpha_kernel(places, p0, p1, p2, g0, g1, g2, constants, after, alpha, token, mixed):
    columns = g0.shape[1]
    matrix = jnp.concatenate([constants[places[1, name]] for name in "boa"], axis=1)
    mixed_pairs((p0, p1, p2), (g0, g1, g2), matrix, mixed)
    for pair in range(mixed.shape[0]):
        spread = across_columns(pair, mixed, constants[places[1, "h"]], constants[places[1, "l"]])
        alpha[2 * pair] = spread[:, :columns]
        alpha[2 * pair + 1] = spread[:, columns:]
    token[...] = jnp.zeros(token.shape, F32)


def scalars_kernel(*refs):
    *messages, once, half0, precision, c_rows, after, scalars, halves = refs
    lines = once.shape[0]
    z2 = sum(message[:lines] for message in messages)
    halves[0] = half0[...]
    halves[1] = sum(message[lines:] for message in messages)
    z1 = once[...]
    rho = precision[...]
    c = c_rows[...]

    def total(x):
        return jnp.sum(jnp.sum(x, axis=0, keepdims=True), axis=1, keepdims=True)

    d = c + rho * z1
    e = z1 + z2
    size = total(d * d)
    shift = jnp.where(size > 0.0, total(c * d) / jnp.where(size > 0.0, size, 1.0), 0.0)
    v = c - shift * d
    w = z1 - shift * e
    values = [
        shift,
        total(c * z1),
        total(d * z1),
        total(v * w),
        total(v * e + d * w),
        total(d * e),
        total(v * z1 + c * w),
        total(d * z1 + c * e),
        total(rho * w * w),
        total(rho * w * e),
        total(rho * e * e),
        total(rho * w * z1),
        total(rho * e * z1),
        total(rho * z1 * z1),
    ]
    lane = lax.broadcasted_iota(jnp.int32, (1, scalars.shape[1]), 1)
    line = jnp.zeros((1, scalars.shape[1]), F32)
    for i, value in enumerate(values):
        line = jnp.where(lane == i, value, line)
    scalars[...] = jnp.broadcast_to(line, scalars.shape)


def combination(scalars):
    table = scalars[...]

    def column(i):
        return table[:, i : i + 1]

    def total(x):
        return jnp.sum(x, axis=0, keepdims=True)

    cz = total(column(1))
    step0 = cz / total(column(2))
    delta = step0 - column(0)
    rr1 = total(column(3) - delta * column(4) + delta * delta * column(5))
    beta = rr1 / cz
    pq1 = rr1 + beta * total(column(6) - delta * column(7)) + beta * beta * cz
    pq1 = pq1 + total(column(8) - 2.0 * delta * column(9) + delta * delta * column(10))
    pq1 = pq1 + 2.0 * beta * total(column(11) - delta * column(12)) + beta * beta * total(column(13))
    step1 = rr1 / pq1
    return step0 + step1 * (1.0 - step0 + beta), -step1 * step0


def final_kernel(place, scalars, alpha0, alpha1, mine, other, alpha, increment):
    first, second = combination(scalars)
    for member in range(alpha.shape[0]):
        alpha[member] = first * alpha0[member] + second * alpha1[member]
    core = lax.rem(place[0], CORES)
    half = mine.shape[1]
    for part, at in ((mine, core), (other, 1 - core)):
        increment[pl.ds(pl.multiple_of(at * half, half), half)] = first * part[0] + second * part[1]


def in_vmem(x):
    return x, pl.BlockSpec(memory_space=pltpu.VMEM)


def in_smem(x):
    return x, pl.BlockSpec(memory_space=pltpu.SMEM)


def anywhere(x):
    return x, pl.BlockSpec(memory_space=pl.ANY)


def call(kernel, outs, args, scratch=()):
    single = not isinstance(outs, list)
    shapes = [jax.ShapeDtypeStruct(shape, F32) for shape in ([outs] if single else outs)]
    out_spec = pl.BlockSpec(memory_space=pltpu.VMEM)
    return pl.pallas_call(
        kernel,
        out_shape=shapes[0] if single else shapes,
        in_specs=[spec for _, spec in args],
        out_specs=out_spec if single else [out_spec] * len(shapes),
        scratch_shapes=list(scratch),
        compiler_params=pltpu.CompilerParams(vmem_limit_bytes=VMEM_LIMIT),
    )(*[x for x, _ in args])


def neighbours(x):
    size = lax.axis_size("tile")
    up = [(i, (i + 1) % size) for i in range(size)]
    down = [(j, i) for i, j in up]
    return lax.ppermute(x, "tile", up), lax.ppermute(x, "tile", down)


def local(perturbations, innovations, obs_precision, obs_weights, obs_cell, obs_count):
    members, levels, rows, columns = perturbations.shape
    slots = obs_cell.shape[0]
    cells = levels * rows
    ens, tiles = lax.axis_size("ens"), lax.axis_size("tile")
    constants = Constants(levels, rows, columns, ens * members)
    places = constants.places
    constants = jnp.asarray(constants.array)
    lines = slots // 128
    p = perturbations.reshape(members, cells, columns)
    cell = obs_cell.reshape(1, slots)
    precision = obs_precision.reshape(1, slots)
    innovations_line = innovations.reshape(1, slots)
    shape = (rows, columns)

    def bound(kernel, *values):
        def run(*refs):
            kernel(*values, *refs)

        return run

    field_shape = (cells, columns)
    half = cells // CORES
    chips = ens // CORES
    place = lax.axis_index("ens").reshape(1)
    vmem = lambda *xs: [in_vmem(x) for x in xs]

    mixed = pltpu.VMEM((members // 2, 2 * cells, CORES * columns), BF16)

    def own_and_after(g, g_after):
        part = call(bound(own_kernel, places), field_shape, vmem(p, g, constants), [mixed])
        return call(bound(side_kernel, places), field_shape, vmem(p, p_after, g_after, part, constants), [mixed])

    def other_core(x):
        return lax.ppermute(x, "ens", [(i, i ^ 1) for i in range(ens)])

    def from_chips(x):
        arrived = [x]
        for back in range(1, chips):
            route = [(c * CORES + core, (c + back) % chips * CORES + core) for c in range(chips) for core in range(CORES)]
            arrived.append(lax.ppermute(x, "ens", route))
        return arrived

    def summed(first, second):
        return call(sum_kernel, first.shape, vmem(first, second))

    def alpha_of(g, g_before, g_after, after):
        return call(
            bound(alpha_kernel, places), [(members, cells, columns), (8, 128)],
            vmem(p_before, p, p_after, g_before, g, g_after, constants) + [anywhere(after)], [mixed],
        )

    p_before, p_after = neighbours(p)
    weights = obs_weights
    g0, precision_rows, c_rows = call(
        bound(start_kernel, *shape), [field_shape, (lines, 128), (lines, 128)],
        [in_smem(obs_count), in_smem(place)] + vmem(weights, cell, precision, innovations_line),
    )
    g0_before, g0_after = neighbours(g0)
    part = own_and_after(g0, g0_after)
    message = (lines + half, columns)
    kept, given = call(
        bound(observe_kernel, *shape, places), [message, message],
        [in_smem(obs_count), in_smem(place)] + vmem(p, p_before, g0_before, part, constants, weights, cell),
        [pltpu.VMEM(field_shape, F32), mixed],
    )
    sent = summed(kept, other_core(given))
    messages = from_chips(sent)
    alpha0, done0 = alpha_of(g0, g0_before, g0_after, sent)
    g1, once, half0 = call(
        bound(middle_kernel, *shape), [field_shape, (lines, 128), (half, columns)],
        [in_smem(obs_count)] + vmem(*messages, weights, cell, precision) + [anywhere(done0)],
    )
    g1_before, g1_after = neighbours(g1)
    part = own_and_after(g1, g1_after)
    kept, given = call(
        bound(observe_kernel, *shape, places), [message, message],
        [in_smem(obs_count), in_smem(place)] + vmem(p, p_before, g1_before, part, constants, weights, cell),
        [pltpu.VMEM(field_shape, F32), mixed],
    )
    sent = summed(kept, other_core(given))
    messages = from_chips(sent)
    alpha1, done1 = alpha_of(g1, g1_before, g1_after, sent)
    scalars, mine = call(
        scalars_kernel, [(tiles, 128), (2, half, columns)],
        vmem(*messages, once, half0, precision_rows, c_rows) + [anywhere(done1)],
    )
    other = other_core(mine)
    scalars = lax.all_to_all(scalars.reshape(tiles, 1, 128), "tile", 0, 0).reshape(tiles, 128)
    alpha, increment = call(
        final_kernel, [(members, cells, columns), field_shape],
        [in_smem(place)] + vmem(scalars, alpha0, alpha1, mine, other),
    )
    return alpha.reshape(perturbations.shape), increment.reshape(levels, rows, columns)


def solution(mesh):
    placed = (
        P("ens", None, "tile", None),
        P("tile"),
        P("tile"),
        P(None, "tile"),
        P("tile"),
        P("tile"),
    )
    return jax.shard_map(
        local,
        mesh=mesh,
        in_specs=placed,
        out_specs=(P("ens", None, "tile", None), P(None, "tile", None)),
        check_vma=False,
    )
```

```python
import math

import jax
import jax.numpy as jnp
import numpy as np
from jax import lax
from jax.experimental import pallas as pl
from jax.experimental.pallas import tpu as pltpu
from jax.sharding import PartitionSpec as P

F32 = jnp.float32
BF16 = jnp.bfloat16
VERTICAL_SPREAD = 2.0
CORES = 2
VMEM_LIMIT = 12 * 1024 * 1024


def gauss(radius, spread):
    offsets = np.arange(-radius, radius + 1) / spread
    return np.exp(-offsets * offsets)


def band(length, spread):
    position = np.arange(length)
    spacing = (position[:, None] - position[None, :]) / spread
    return np.exp(-spacing * spacing) / np.sqrt(np.sum(gauss(length, spread) ** 2))


def bf16_pair(matrix):
    matrix = matrix.astype(np.float32)
    high = matrix.astype(jnp.bfloat16)
    low = (matrix - high.astype(np.float32)).astype(jnp.bfloat16)
    return high, low


def local_matrices(levels, rows, columns, power, scale):
    radius = rows // 2
    kernel = gauss(radius, float(radius))
    kernel = kernel / np.sqrt(np.sum(kernel * kernel))
    vertical = band(levels, VERTICAL_SPREAD)
    lateral = band(columns, columns / 16.0)
    if power == 2:
        kernel = np.convolve(kernel, kernel)
        vertical = vertical @ vertical
        lateral = lateral @ lateral
    reach = (len(kernel) - 1) // 2
    blocks = []
    for tile in (-1, 0, 1):
        offset = tile * rows + np.arange(rows)[None, :] - np.arange(rows)[:, None]
        inside = np.abs(offset) <= reach
        along = np.where(inside, kernel[np.clip(offset + reach, 0, 2 * reach)], 0.0)
        blocks.append(np.concatenate(bf16_pair(np.kron(vertical, along) * scale)))
    high, low = bf16_pair(lateral)
    return blocks, np.block([[high, low], [high, np.zeros_like(low)]])


class Constants:
    def __init__(self, levels, rows, columns, members):
        self.places, arrays, start = {}, [], 0
        for power in (2, 1):
            blocks, across = local_matrices(levels, rows, columns, power, float(members) ** (-power / 2))
            for name, array in list(zip("boa", blocks)) + [("y", across)]:
                self.places[power, name] = slice(start, start + array.shape[0])
                arrays.append(array)
                start += array.shape[0]
        self.array = np.concatenate(arrays)


def split(x):
    high = x.astype(BF16)
    return high, (x - high.astype(F32)).astype(BF16)


def dot(a, b):
    return jnp.dot(a, b, preferred_element_type=F32)


def column_hits(cell, columns):
    return jnp.where(
        lax.broadcasted_iota(jnp.int32, (columns, cell.shape[1]), 0) == cell % columns, 1.0, 0.0
    ).astype(BF16)


def adjoint(values, weights_ref, cell_ref, rows, columns):
    levels, slots = weights_ref.shape
    total = levels * rows
    chunk = 256
    field = jnp.zeros((2 * total, columns), F32)
    for start in range(0, slots, chunk):
        cell = cell_ref[:, start : start + chunk]
        hits = column_hits(cell, columns)
        here = lax.broadcasted_iota(jnp.int32, (rows, chunk), 0) == cell // columns
        weighted = weights_ref[:, start : start + chunk] * values[:, start : start + chunk]
        parts = [jnp.where(here, weighted[level : level + 1], 0.0) for level in range(levels)]
        high, low = split(jnp.concatenate(parts, axis=0))
        both = jnp.concatenate([high, low], axis=0)
        field = field + lax.dot_general(both, hits, (((1,), (1,)), ((), ())), preferred_element_type=F32)
    return field[:total] + field[total:]


def observe(field, weights_ref, cell_ref, live, rows, columns):
    levels, slots = weights_ref.shape
    chunk = 256
    high, low = split(field)
    both = jnp.concatenate([high, low], axis=1)
    observed = []
    for start in range(0, slots, chunk):
        cell = cell_ref[:, start : start + chunk]
        hits = column_hits(cell, columns)
        picked = dot(both, jnp.concatenate([hits, hits], axis=0))
        here = lax.broadcasted_iota(jnp.int32, (rows, chunk), 0) == cell // columns
        total = jnp.zeros((rows, chunk), F32)
        for level in range(levels):
            weight = weights_ref[level : level + 1, start : start + chunk]
            total = total + jnp.where(here, picked[level * rows : (level + 1) * rows], 0.0) * weight
        observed.append(jnp.sum(total, axis=0, keepdims=True))
    return jnp.concatenate(observed, axis=1) * live


def live_slots(count_ref, slots):
    return jnp.where(lax.broadcasted_iota(jnp.int32, (1, slots), 1) < count_ref[0], 1.0, 0.0)


def mix_rows(p_refs, g_refs, rows_matrix, mixed):
    total, columns = g_refs[0].shape
    for first in range(0, mixed.shape[0], 2):
        sides = []
        for member in (first, first + 1):
            sides.append(jnp.concatenate([p[member].astype(F32) * g[...] for p, g in zip(p_refs, g_refs)], axis=0))
        high, low = split(jnp.concatenate(sides, axis=1))
        product = dot(rows_matrix, high)
        high, low = split(product[:total] + product[total:] + dot(rows_matrix[:total], low))
        for i in range(2):
            lanes = slice(i * columns, (i + 1) * columns)
            mixed[first + i, :, :columns] = high[:, lanes]
            mixed[first + i, :, columns:] = low[:, lanes]


def across_columns(member, mixed, matrix):
    product = dot(mixed[member], matrix)
    columns = product.shape[1] // 2
    return product[:, :columns] + product[:, columns:]


def summed_members(field, weigh, p_side, g_side, constants, places, which, mixed):
    mix_rows([p_side], [g_side], constants[places[2, which]], mixed)
    for member in range(mixed.shape[0]):
        field = field + weigh[member].astype(F32) * across_columns(member, mixed, constants[places[2, "y"]])
    return field


def as_rows(line, width=128):
    return jnp.concatenate([line[:, i : i + width] for i in range(0, line.shape[1], width)], axis=0)


def as_line(block):
    return jnp.concatenate([block[i : i + 1] for i in range(block.shape[0])], axis=1)


def start_kernel(rows, columns, count, place, weights, cell, precision, innovations, field, precision_rows, c_rows):
    c = live_slots(count, weights.shape[1]) * precision[...] * innovations[...]
    field[...] = adjoint(c, weights, cell, rows, columns)
    precision_rows[...] = as_rows(precision[...])
    c_rows[...] = as_rows(c)


def own_kernel(places, p, g, constants, field, mixed):
    field[...] = summed_members(jnp.zeros(g.shape, F32), p, p, g, constants, places, "o", mixed)


def side_kernel(places, p, p_side, g_side, part, constants, field, mixed):
    field[...] = summed_members(part[...], p, p_side, g_side, constants, places, "a", mixed)


def message_rows(place, observed, field, kept, given):
    lines = observed.shape[0]
    half = field.shape[0] // CORES
    core = lax.rem(place[0], CORES)
    for message, at in ((kept, core), (given, 1 - core)):
        message[:lines] = observed
        message[lines:] = field[pl.ds(pl.multiple_of(at * half, half), half)]


def observe_kernel(rows, columns, places, count, place, p, p_side, g_side, part, constants, weights, cell, kept, given, field, mixed):
    field[...] = summed_members(part[...], p, p_side, g_side, constants, places, "b", mixed)
    observed = as_rows(observe(field[...], weights, cell, live_slots(count, weights.shape[1]), rows, columns))
    message_rows(place, observed, field, kept, given)


def sum_kernel(first, second, total):
    total[...] = first[...] + second[...]


def middle_kernel(rows, columns, count, *refs):
    *messages, weights, cell, precision, after, field, observed, half = refs
    lines = observed.shape[0]
    half[...] = sum(message[lines:] for message in messages)
    summed = sum(message[:lines] for message in messages)
    observed[...] = summed
    field[...] = adjoint(precision[...] * as_line(summed), weights, cell, rows, columns)


def alpha_kernel(places, p0, p1, p2, g0, g1, g2, constants, after, alpha, token, mixed):
    matrix = jnp.concatenate([constants[places[1, name]] for name in "boa"], axis=1)
    mix_rows((p0, p1, p2), (g0, g1, g2), matrix, mixed)
    for member in range(mixed.shape[0]):
        alpha[member] = across_columns(member, mixed, constants[places[1, "y"]])
    token[...] = jnp.zeros(token.shape, F32)


def scalars_kernel(*refs):
    *messages, once, half0, precision, c_rows, after, scalars, halves = refs
    lines = once.shape[0]
    z2 = sum(message[:lines] for message in messages)
    halves[0] = half0[...]
    halves[1] = sum(message[lines:] for message in messages)
    z1 = once[...]
    rho = precision[...]
    c = c_rows[...]

    def total(x):
        return jnp.sum(jnp.sum(x, axis=0, keepdims=True), axis=1, keepdims=True)

    d = c + rho * z1
    e = z1 + z2
    size = total(d * d)
    shift = jnp.where(size > 0.0, total(c * d) / jnp.where(size > 0.0, size, 1.0), 0.0)
    v = c - shift * d
    w = z1 - shift * e
    values = [
        shift,
        total(c * z1),
        total(d * z1),
        total(v * w),
        total(v * e + d * w),
        total(d * e),
        total(v * z1 + c * w),
        total(d * z1 + c * e),
        total(rho * w * w),
        total(rho * w * e),
        total(rho * e * e),
        total(rho * w * z1),
        total(rho * e * z1),
        total(rho * z1 * z1),
    ]
    lane = lax.broadcasted_iota(jnp.int32, (1, scalars.shape[1]), 1)
    line = jnp.zeros((1, scalars.shape[1]), F32)
    for i, value in enumerate(values):
        line = jnp.where(lane == i, value, line)
    scalars[...] = jnp.broadcast_to(line, scalars.shape)


def combination(scalars):
    table = scalars[...]

    def column(i):
        return table[:, i : i + 1]

    def total(x):
        return jnp.sum(x, axis=0, keepdims=True)

    cz = total(column(1))
    step0 = cz / total(column(2))
    delta = step0 - column(0)
    rr1 = total(column(3) - delta * column(4) + delta * delta * column(5))
    beta = rr1 / cz
    pq1 = rr1 + beta * total(column(6) - delta * column(7)) + beta * beta * cz
    pq1 = pq1 + total(column(8) - 2.0 * delta * column(9) + delta * delta * column(10))
    pq1 = pq1 + 2.0 * beta * total(column(11) - delta * column(12)) + beta * beta * total(column(13))
    step1 = rr1 / pq1
    return step0 + step1 * (1.0 - step0 + beta), -step1 * step0


def final_kernel(place, scalars, alpha0, alpha1, mine, other, alpha_out, increment_out, alpha, increment, sems):
    first, second = combination(scalars)
    core = lax.rem(place[0], CORES)
    half = mine.shape[1]
    for part, at in ((mine, core), (other, 1 - core)):
        increment[pl.ds(pl.multiple_of(at * half, half), half)] = first * part[0] + second * part[1]
    copies = [pltpu.make_async_copy(increment, increment_out, sems.at[0])]
    copies[0].start()
    for member in range(0, alpha.shape[0], 2):
        pair = pl.ds(member, 2)
        alpha[pair] = first * alpha0[pair] + second * alpha1[pair]
        copies.append(pltpu.make_async_copy(alpha.at[pair], alpha_out.at[pair], sems.at[1 + member // 2]))
        copies[-1].start()
    for copy in copies:
        copy.wait()


def in_vmem(x):
    return x, pl.BlockSpec(memory_space=pltpu.VMEM)


def in_smem(x):
    return x, pl.BlockSpec(memory_space=pltpu.SMEM)


def anywhere(x):
    return x, pl.BlockSpec(memory_space=pl.ANY)


def call(kernel, outs, args, scratch=(), out_space=pltpu.VMEM):
    single = not isinstance(outs, list)
    shapes = [jax.ShapeDtypeStruct(shape, F32) for shape in ([outs] if single else outs)]
    out_spec = pl.BlockSpec(memory_space=out_space)
    return pl.pallas_call(
        kernel,
        out_shape=shapes[0] if single else shapes,
        in_specs=[spec for _, spec in args],
        out_specs=out_spec if single else [out_spec] * len(shapes),
        scratch_shapes=list(scratch),
        compiler_params=pltpu.CompilerParams(vmem_limit_bytes=VMEM_LIMIT),
    )(*[x for x, _ in args])


def neighbours(x):
    size = lax.axis_size("tile")
    up = [(i, (i + 1) % size) for i in range(size)]
    down = [(j, i) for i, j in up]
    return lax.ppermute(x, "tile", up), lax.ppermute(x, "tile", down)


def local(perturbations, innovations, obs_precision, obs_weights, obs_cell, obs_count):
    members, levels, rows, columns = perturbations.shape
    slots = obs_cell.shape[0]
    cells = levels * rows
    ens, tiles = lax.axis_size("ens"), lax.axis_size("tile")
    constants = Constants(levels, rows, columns, ens * members)
    places = constants.places
    constants = jnp.asarray(constants.array)
    lines = slots // 128
    p = perturbations.reshape(members, cells, columns)
    cell = obs_cell.reshape(1, slots)
    precision = obs_precision.reshape(1, slots)
    innovations_line = innovations.reshape(1, slots)
    shape = (rows, columns)

    def bound(kernel, *values):
        def run(*refs):
            kernel(*values, *refs)

        return run

    field_shape = (cells, columns)
    half = cells // CORES
    chips = ens // CORES
    place = lax.axis_index("ens").reshape(1)
    vmem = lambda *xs: [in_vmem(x) for x in xs]

    mixed = pltpu.VMEM((members, cells, 2 * columns), BF16)

    def own_and_after(g, g_after):
        part = call(bound(own_kernel, places), field_shape, vmem(p, g, constants), [mixed])
        return call(bound(side_kernel, places), field_shape, vmem(p, p_after, g_after, part, constants), [mixed])

    def other_core(x):
        return lax.ppermute(x, "ens", [(i, i ^ 1) for i in range(ens)])

    def from_chips(x):
        arrived = [x]
        for back in range(1, chips):
            route = [(c * CORES + core, (c + back) % chips * CORES + core) for c in range(chips) for core in range(CORES)]
            arrived.append(lax.ppermute(x, "ens", route))
        return arrived

    def summed(first, second):
        return call(sum_kernel, first.shape, vmem(first, second))

    def alpha_of(g, g_before, g_after, after):
        return call(
            bound(alpha_kernel, places), [(members, cells, columns), (8, 128)],
            vmem(p_before, p, p_after, g_before, g, g_after, constants) + [anywhere(after)], [mixed],
        )

    p_before, p_after = neighbours(p)
    weights = obs_weights
    g0, precision_rows, c_rows = call(
        bound(start_kernel, *shape), [field_shape, (lines, 128), (lines, 128)],
        [in_smem(obs_count), in_smem(place)] + vmem(weights, cell, precision, innovations_line),
    )
    g0_before, g0_after = neighbours(g0)
    part = own_and_after(g0, g0_after)
    message = (lines + half, columns)
    kept, given = call(
        bound(observe_kernel, *shape, places), [message, message],
        [in_smem(obs_count), in_smem(place)] + vmem(p, p_before, g0_before, part, constants, weights, cell),
        [pltpu.VMEM(field_shape, F32), mixed],
    )
    sent = summed(kept, other_core(given))
    messages = from_chips(sent)
    alpha0, done0 = alpha_of(g0, g0_before, g0_after, sent)
    g1, once, half0 = call(
        bound(middle_kernel, *shape), [field_shape, (lines, 128), (half, columns)],
        [in_smem(obs_count)] + vmem(*messages, weights, cell, precision) + [anywhere(done0)],
    )
    g1_before, g1_after = neighbours(g1)
    part = own_and_after(g1, g1_after)
    kept, given = call(
        bound(observe_kernel, *shape, places), [message, message],
        [in_smem(obs_count), in_smem(place)] + vmem(p, p_before, g1_before, part, constants, weights, cell),
        [pltpu.VMEM(field_shape, F32), mixed],
    )
    sent = summed(kept, other_core(given))
    messages = from_chips(sent)
    alpha1, done1 = alpha_of(g1, g1_before, g1_after, sent)
    scalars, mine = call(
        scalars_kernel, [(tiles, 128), (2, half, columns)],
        vmem(*messages, once, half0, precision_rows, c_rows) + [anywhere(done1)],
    )
    other = other_core(mine)
    scalars = lax.all_to_all(scalars.reshape(tiles, 1, 128), "tile", 0, 0).reshape(tiles, 128)
    alpha, increment = call(
        final_kernel, [(members, cells, columns), field_shape],
        [in_smem(place)] + vmem(scalars, alpha0, alpha1, mine, other),
        [pltpu.VMEM((members, cells, columns), F32), pltpu.VMEM(field_shape, F32), pltpu.SemaphoreType.DMA((members,))],
        out_space=pl.ANY,
    )
    return alpha.reshape(perturbations.shape), increment.reshape(levels, rows, columns)


def solution(mesh):
    placed = (
        P("ens", None, "tile", None),
        P("tile"),
        P("tile"),
        P(None, "tile"),
        P("tile"),
        P("tile"),
    )
    return jax.shard_map(
        local,
        mesh=mesh,
        in_specs=placed,
        out_specs=(P("ens", None, "tile", None), P(None, "tile", None)),
        check_vma=False,
    )
```

```python
import math

import jax
import jax.numpy as jnp
import numpy as np
from jax import lax
from jax.experimental import pallas as pl
from jax.experimental.pallas import tpu as pltpu
from jax.sharding import PartitionSpec as P

F32 = jnp.float32
BF16 = jnp.bfloat16
VERTICAL_SPREAD = 2.0
CORES = 2
VMEM_LIMIT = 12 * 1024 * 1024


def gauss(radius, spread):
    offsets = np.arange(-radius, radius + 1) / spread
    return np.exp(-offsets * offsets)


def band(length, spread):
    position = np.arange(length)
    spacing = (position[:, None] - position[None, :]) / spread
    return np.exp(-spacing * spacing) / np.sqrt(np.sum(gauss(length, spread) ** 2))


def bf16_pair(matrix):
    matrix = matrix.astype(np.float32)
    high = matrix.astype(jnp.bfloat16)
    low = (matrix - high.astype(np.float32)).astype(jnp.bfloat16)
    return high, low


def local_matrices(levels, rows, columns, power, scale):
    radius = rows // 2
    kernel = gauss(radius, float(radius))
    kernel = kernel / np.sqrt(np.sum(kernel * kernel))
    vertical = band(levels, VERTICAL_SPREAD)
    lateral = band(columns, columns / 16.0)
    if power == 2:
        kernel = np.convolve(kernel, kernel)
        vertical = vertical @ vertical
        lateral = lateral @ lateral
    reach = (len(kernel) - 1) // 2
    blocks = []
    for tile in (-1, 0, 1):
        offset = tile * rows + np.arange(rows)[None, :] - np.arange(rows)[:, None]
        inside = np.abs(offset) <= reach
        along = np.where(inside, kernel[np.clip(offset + reach, 0, 2 * reach)], 0.0)
        blocks.append(np.concatenate(bf16_pair(np.kron(vertical, along) * scale)))
    high, low = bf16_pair(lateral)
    return blocks, np.block([[high, low], [high, np.zeros_like(low)]])


class Constants:
    def __init__(self, levels, rows, columns, members):
        self.places, arrays, start = {}, [], 0
        for power in (2, 1):
            blocks, across = local_matrices(levels, rows, columns, power, float(members) ** (-power / 2))
            for name, array in list(zip("boa", blocks)) + [("y", across)]:
                self.places[power, name] = slice(start, start + array.shape[0])
                arrays.append(array)
                start += array.shape[0]
        self.array = np.concatenate(arrays)


def split(x):
    high = x.astype(BF16)
    return high, (x - high.astype(F32)).astype(BF16)


def dot(a, b):
    return jnp.dot(a, b, preferred_element_type=F32)


def column_hits(cell, columns):
    return jnp.where(
        lax.broadcasted_iota(jnp.int32, (columns, cell.shape[1]), 0) == cell % columns, 1.0, 0.0
    ).astype(BF16)


def adjoint(values, weights_ref, cell_ref, rows, columns):
    levels, slots = weights_ref.shape
    total = levels * rows
    chunk = 256
    field = jnp.zeros((2 * total, columns), F32)
    for start in range(0, slots, chunk):
        cell = cell_ref[:, start : start + chunk]
        hits = column_hits(cell, columns)
        here = lax.broadcasted_iota(jnp.int32, (rows, chunk), 0) == cell // columns
        weighted = weights_ref[:, start : start + chunk] * values[:, start : start + chunk]
        parts = [jnp.where(here, weighted[level : level + 1], 0.0) for level in range(levels)]
        high, low = split(jnp.concatenate(parts, axis=0))
        both = jnp.concatenate([high, low], axis=0)
        field = field + lax.dot_general(both, hits, (((1,), (1,)), ((), ())), preferred_element_type=F32)
    return field[:total] + field[total:]


def observe(field, weights_ref, cell_ref, live, rows, columns):
    levels, slots = weights_ref.shape
    chunk = 256
    high, low = split(field)
    both = jnp.concatenate([high, low], axis=1)
    observed = []
    for start in range(0, slots, chunk):
        cell = cell_ref[:, start : start + chunk]
        hits = column_hits(cell, columns)
        picked = dot(both, jnp.concatenate([hits, hits], axis=0))
        here = lax.broadcasted_iota(jnp.int32, (rows, chunk), 0) == cell // columns
        total = jnp.zeros((rows, chunk), F32)
        for level in range(levels):
            weight = weights_ref[level : level + 1, start : start + chunk]
            total = total + jnp.where(here, picked[level * rows : (level + 1) * rows], 0.0) * weight
        observed.append(jnp.sum(total, axis=0, keepdims=True))
    return jnp.concatenate(observed, axis=1) * live


def live_slots(count_ref, slots):
    return jnp.where(lax.broadcasted_iota(jnp.int32, (1, slots), 1) < count_ref[0], 1.0, 0.0)


def mix_rows(p_refs, g_refs, rows_matrix, mixed):
    total, columns = g_refs[0].shape
    for first in range(0, mixed.shape[0], 2):
        sides = []
        for member in (first, first + 1):
            sides.append(jnp.concatenate([p[member].astype(F32) * g[...] for p, g in zip(p_refs, g_refs)], axis=0))
        high, low = split(jnp.concatenate(sides, axis=1))
        product = dot(rows_matrix, high)
        high, low = split(product[:total] + product[total:] + dot(rows_matrix[:total], low))
        for i in range(2):
            lanes = slice(i * columns, (i + 1) * columns)
            mixed[first + i, :, :columns] = high[:, lanes]
            mixed[first + i, :, columns:] = low[:, lanes]


def across_columns(member, mixed, matrix):
    product = dot(mixed[member], matrix)
    columns = product.shape[1] // 2
    return product[:, :columns] + product[:, columns:]


def summed_members(field, weigh, p_side, g_side, constants, places, which, mixed):
    mix_rows([p_side], [g_side], constants[places[2, which]], mixed)
    for member in range(mixed.shape[0]):
        field = field + weigh[member].astype(F32) * across_columns(member, mixed, constants[places[2, "y"]])
    return field


def as_rows(line, width=128):
    return jnp.concatenate([line[:, i : i + width] for i in range(0, line.shape[1], width)], axis=0)


def as_line(block):
    return jnp.concatenate([block[i : i + 1] for i in range(block.shape[0])], axis=1)


def start_kernel(rows, columns, count, place, weights, cell, precision, innovations, field, precision_rows, c_rows):
    c = live_slots(count, weights.shape[1]) * precision[...] * innovations[...]
    field[...] = adjoint(c, weights, cell, rows, columns)
    precision_rows[...] = as_rows(precision[...])
    c_rows[...] = as_rows(c)


def own_kernel(places, p, g, constants, field, mixed):
    field[...] = summed_members(jnp.zeros(g.shape, F32), p, p, g, constants, places, "o", mixed)


def side_kernel(places, p, p_side, g_side, part, constants, field, mixed):
    field[...] = summed_members(part[...], p, p_side, g_side, constants, places, "a", mixed)


def message_rows(place, observed, field, kept, given):
    lines = observed.shape[0]
    half = field.shape[0] // CORES
    core = lax.rem(place[0], CORES)
    for message, at in ((kept, core), (given, 1 - core)):
        message[:lines] = observed
        message[lines:] = field[pl.ds(pl.multiple_of(at * half, half), half)]


def observe_kernel(rows, columns, places, count, place, p, p_side, g_side, part, constants, weights, cell, kept, given, field, mixed):
    field[...] = summed_members(part[...], p, p_side, g_side, constants, places, "b", mixed)
    observed = as_rows(observe(field[...], weights, cell, live_slots(count, weights.shape[1]), rows, columns))
    message_rows(place, observed, field, kept, given)


def sum_kernel(first, second, total):
    total[...] = first[...] + second[...]


def middle_kernel(rows, columns, count, *refs):
    *messages, weights, cell, precision, after, field, observed, half = refs
    lines = observed.shape[0]
    half[...] = sum(message[lines:] for message in messages)
    summed = sum(message[:lines] for message in messages)
    observed[...] = summed
    field[...] = adjoint(precision[...] * as_line(summed), weights, cell, rows, columns)


def alpha_kernel(places, p0, p1, p2, g0, g1, g2, constants, after, alpha, token, mixed):
    matrix = jnp.concatenate([constants[places[1, name]] for name in "boa"], axis=1)
    mix_rows((p0, p1, p2), (g0, g1, g2), matrix, mixed)
    for member in range(mixed.shape[0]):
        alpha[member] = across_columns(member, mixed, constants[places[1, "y"]])
    token[...] = jnp.zeros(token.shape, F32)


def scalars_kernel(*refs):
    *messages, once, half0, precision, c_rows, after, scalars, halves = refs
    lines = once.shape[0]
    z2 = sum(message[:lines] for message in messages)
    halves[0] = half0[...]
    halves[1] = sum(message[lines:] for message in messages)
    z1 = once[...]
    rho = precision[...]
    c = c_rows[...]

    def total(x):
        return jnp.sum(jnp.sum(x, axis=0, keepdims=True), axis=1, keepdims=True)

    d = c + rho * z1
    e = z1 + z2
    size = total(d * d)
    shift = jnp.where(size > 0.0, total(c * d) / jnp.where(size > 0.0, size, 1.0), 0.0)
    shift = jnp.clip(shift, 0.0, 1.0)
    v = c - shift * d
    w = z1 - shift * e
    values = [
        shift,
        total(c * z1),
        total(d * z1),
        total(v * w),
        total(v * e + d * w),
        total(d * e),
        total(v * z1 + c * w),
        total(d * z1 + c * e),
        total(rho * w * w),
        total(rho * w * e),
        total(rho * e * e),
        total(rho * w * z1),
        total(rho * e * z1),
        total(rho * z1 * z1),
    ]
    lane = lax.broadcasted_iota(jnp.int32, (1, scalars.shape[1]), 1)
    line = jnp.zeros((1, scalars.shape[1]), F32)
    for i, value in enumerate(values):
        line = jnp.where(lane == i, value, line)
    scalars[...] = jnp.broadcast_to(line, scalars.shape)


def combination(scalars):
    table = scalars[...]

    def column(i):
        return table[:, i : i + 1]

    def total(x):
        return jnp.sum(x, axis=0, keepdims=True)

    cz = total(column(1))
    step0 = cz / total(column(2))
    delta = step0 - column(0)
    rr1 = total(column(3) - delta * column(4) + delta * delta * column(5))
    beta = rr1 / cz
    pq1 = rr1 + beta * total(column(6) - delta * column(7)) + beta * beta * cz
    pq1 = pq1 + total(column(8) - 2.0 * delta * column(9) + delta * delta * column(10))
    pq1 = pq1 + 2.0 * beta * total(column(11) - delta * column(12)) + beta * beta * total(column(13))
    step1 = rr1 / pq1
    return step0 + step1 * (1.0 - step0 + beta), -step1 * step0


def final_kernel(place, scalars, alpha0, alpha1, mine, other, alpha_out, increment_out, alpha, increment, sems):
    first, second = combination(scalars)
    core = lax.rem(place[0], CORES)
    half = mine.shape[1]
    for part, at in ((mine, core), (other, 1 - core)):
        increment[pl.ds(pl.multiple_of(at * half, half), half)] = first * part[0] + second * part[1]
    copies = [pltpu.make_async_copy(increment, increment_out, sems.at[0])]
    copies[0].start()
    for member in range(0, alpha.shape[0], 2):
        pair = pl.ds(member, 2)
        alpha[pair] = first * alpha0[pair] + second * alpha1[pair]
        copies.append(pltpu.make_async_copy(alpha.at[pair], alpha_out.at[pair], sems.at[1 + member // 2]))
        copies[-1].start()
    for copy in copies:
        copy.wait()


def in_vmem(x):
    return x, pl.BlockSpec(memory_space=pltpu.VMEM)


def in_smem(x):
    return x, pl.BlockSpec(memory_space=pltpu.SMEM)


def anywhere(x):
    return x, pl.BlockSpec(memory_space=pl.ANY)


def call(kernel, outs, args, scratch=(), out_space=pltpu.VMEM):
    single = not isinstance(outs, list)
    shapes = [jax.ShapeDtypeStruct(shape, F32) for shape in ([outs] if single else outs)]
    out_spec = pl.BlockSpec(memory_space=out_space)
    return pl.pallas_call(
        kernel,
        out_shape=shapes[0] if single else shapes,
        in_specs=[spec for _, spec in args],
        out_specs=out_spec if single else [out_spec] * len(shapes),
        scratch_shapes=list(scratch),
        compiler_params=pltpu.CompilerParams(vmem_limit_bytes=VMEM_LIMIT),
    )(*[x for x, _ in args])


def neighbours(x):
    size = lax.axis_size("tile")
    up = [(i, (i + 1) % size) for i in range(size)]
    down = [(j, i) for i, j in up]
    return lax.ppermute(x, "tile", up), lax.ppermute(x, "tile", down)


def local(perturbations, innovations, obs_precision, obs_weights, obs_cell, obs_count):
    members, levels, rows, columns = perturbations.shape
    slots = obs_cell.shape[0]
    cells = levels * rows
    ens, tiles = lax.axis_size("ens"), lax.axis_size("tile")
    constants = Constants(levels, rows, columns, ens * members)
    places = constants.places
    constants = jnp.asarray(constants.array)
    lines = slots // 128
    p = perturbations.reshape(members, cells, columns)
    cell = obs_cell.reshape(1, slots)
    precision = obs_precision.reshape(1, slots)
    innovations_line = innovations.reshape(1, slots)
    shape = (rows, columns)

    def bound(kernel, *values):
        def run(*refs):
            kernel(*values, *refs)

        return run

    field_shape = (cells, columns)
    half = cells // CORES
    chips = ens // CORES
    place = lax.axis_index("ens").reshape(1)
    vmem = lambda *xs: [in_vmem(x) for x in xs]

    mixed = pltpu.VMEM((members, cells, 2 * columns), BF16)

    def own_and_after(g, g_after):
        part = call(bound(own_kernel, places), field_shape, vmem(p, g, constants), [mixed])
        return call(bound(side_kernel, places), field_shape, vmem(p, p_after, g_after, part, constants), [mixed])

    def other_core(x):
        return lax.ppermute(x, "ens", [(i, i ^ 1) for i in range(ens)])

    def from_chips(x):
        arrived = [x]
        for back in range(1, chips):
            route = [(c * CORES + core, (c + back) % chips * CORES + core) for c in range(chips) for core in range(CORES)]
            arrived.append(lax.ppermute(x, "ens", route))
        return arrived

    def summed(first, second):
        return call(sum_kernel, first.shape, vmem(first, second))

    def alpha_of(g, g_before, g_after, after):
        return call(
            bound(alpha_kernel, places), [(members, cells, columns), (8, 128)],
            vmem(p_before, p, p_after, g_before, g, g_after, constants) + [anywhere(after)], [mixed],
        )

    p_before, p_after = neighbours(p)
    weights = obs_weights
    g0, precision_rows, c_rows = call(
        bound(start_kernel, *shape), [field_shape, (lines, 128), (lines, 128)],
        [in_smem(obs_count), in_smem(place)] + vmem(weights, cell, precision, innovations_line),
    )
    g0_before, g0_after = neighbours(g0)
    part = own_and_after(g0, g0_after)
    message = (lines + half, columns)
    kept, given = call(
        bound(observe_kernel, *shape, places), [message, message],
        [in_smem(obs_count), in_smem(place)] + vmem(p, p_before, g0_before, part, constants, weights, cell),
        [pltpu.VMEM(field_shape, F32), mixed],
    )
    sent = summed(kept, other_core(given))
    messages = from_chips(sent)
    alpha0, done0 = alpha_of(g0, g0_before, g0_after, sent)
    g1, once, half0 = call(
        bound(middle_kernel, *shape), [field_shape, (lines, 128), (half, columns)],
        [in_smem(obs_count)] + vmem(*messages, weights, cell, precision) + [anywhere(done0)],
    )
    g1_before, g1_after = neighbours(g1)
    part = own_and_after(g1, g1_after)
    kept, given = call(
        bound(observe_kernel, *shape, places), [message, message],
        [in_smem(obs_count), in_smem(place)] + vmem(p, p_before, g1_before, part, constants, weights, cell),
        [pltpu.VMEM(field_shape, F32), mixed],
    )
    sent = summed(kept, other_core(given))
    messages = from_chips(sent)
    alpha1, done1 = alpha_of(g1, g1_before, g1_after, sent)
    scalars, mine = call(
        scalars_kernel, [(tiles, 128), (2, half, columns)],
        vmem(*messages, once, half0, precision_rows, c_rows) + [anywhere(done1)],
    )
    other = other_core(mine)
    scalars = lax.all_to_all(scalars.reshape(tiles, 1, 128), "tile", 0, 0).reshape(tiles, 128)
    alpha, increment = call(
        final_kernel, [(members, cells, columns), field_shape],
        [in_smem(place)] + vmem(scalars, alpha0, alpha1, mine, other),
        [pltpu.VMEM((members, cells, columns), F32), pltpu.VMEM(field_shape, F32), pltpu.SemaphoreType.DMA((members,))],
        out_space=pl.ANY,
    )
    return alpha.reshape(perturbations.shape), increment.reshape(levels, rows, columns)


def solution(mesh):
    placed = (
        P("ens", None, "tile", None),
        P("tile"),
        P("tile"),
        P(None, "tile"),
        P("tile"),
        P("tile"),
    )
    return jax.shard_map(
        local,
        mesh=mesh,
        in_specs=placed,
        out_specs=(P("ens", None, "tile", None), P(None, "tile", None)),
        check_vma=False,
    )
```

```python
import math

import jax
import jax.numpy as jnp
import numpy as np
from jax import lax
from jax.experimental import pallas as pl
from jax.experimental.pallas import tpu as pltpu
from jax.sharding import PartitionSpec as P

F32 = jnp.float32
BF16 = jnp.bfloat16
VERTICAL_SPREAD = 2.0
CORES = 2
VMEM_LIMIT = 12 * 1024 * 1024


def gauss(radius, spread):
    offsets = np.arange(-radius, radius + 1) / spread
    return np.exp(-offsets * offsets)


def band(length, spread):
    position = np.arange(length)
    spacing = (position[:, None] - position[None, :]) / spread
    return np.exp(-spacing * spacing) / np.sqrt(np.sum(gauss(length, spread) ** 2))


def bf16_pair(matrix):
    matrix = matrix.astype(np.float32)
    high = matrix.astype(jnp.bfloat16)
    low = (matrix - high.astype(np.float32)).astype(jnp.bfloat16)
    return high, low


def local_matrices(levels, rows, columns, power, scale):
    radius = rows // 2
    kernel = gauss(radius, float(radius))
    kernel = kernel / np.sqrt(np.sum(kernel * kernel))
    vertical = band(levels, VERTICAL_SPREAD)
    lateral = band(columns, columns / 16.0)
    if power == 2:
        kernel = np.convolve(kernel, kernel)
        vertical = vertical @ vertical
        lateral = lateral @ lateral
    reach = (len(kernel) - 1) // 2
    blocks = []
    for tile in (-1, 0, 1):
        offset = tile * rows + np.arange(rows)[None, :] - np.arange(rows)[:, None]
        inside = np.abs(offset) <= reach
        along = np.where(inside, kernel[np.clip(offset + reach, 0, 2 * reach)], 0.0)
        blocks.append(np.concatenate(bf16_pair(np.kron(vertical, along) * scale)))
    high, low = bf16_pair(lateral)
    return blocks, np.block([[high, low], [high, np.zeros_like(low)]])


class Constants:
    def __init__(self, levels, rows, columns, members):
        self.places, arrays, start = {}, [], 0
        for power in (2, 1):
            blocks, across = local_matrices(levels, rows, columns, power, float(members) ** (-power / 2))
            for name, array in list(zip("boa", blocks)) + [("y", across)]:
                self.places[power, name] = slice(start, start + array.shape[0])
                arrays.append(array)
                start += array.shape[0]
        self.array = np.concatenate(arrays)


def split(x):
    high = x.astype(BF16)
    return high, (x - high.astype(F32)).astype(BF16)


def dot(a, b):
    return jnp.dot(a, b, preferred_element_type=F32)


def column_hits(cell, columns):
    column = lax.rem(cell, columns) if columns & (columns - 1) else cell & (columns - 1)
    return jnp.where(lax.broadcasted_iota(jnp.int32, (columns, cell.shape[1]), 0) == column, 1.0, 0.0).astype(BF16)


def row_hits(cell, rows, columns):
    row = lax.div(cell, columns) if columns & (columns - 1) else cell >> (columns.bit_length() - 1)
    return lax.broadcasted_iota(jnp.int32, (rows, cell.shape[1]), 0) == row


def adjoint(values, weights_ref, cell_ref, hits_ref, rows, parts_ref):
    levels, slots = weights_ref.shape
    columns = hits_ref.shape[0]
    total = levels * rows
    chunk = 256
    for start in range(0, slots, chunk):
        lanes = slice(start, start + chunk)
        here = row_hits(cell_ref[:, lanes], rows, columns)
        weighted = weights_ref[:, lanes] * values[:, lanes]
        parts = [jnp.where(here, weighted[level : level + 1], 0.0) for level in range(levels)]
        high, low = split(jnp.concatenate(parts, axis=0))
        parts_ref[:total, lanes] = high
        parts_ref[total:, lanes] = low
    field = lax.dot_general(
        parts_ref[...], hits_ref[...], (((1,), (1,)), ((), ())), preferred_element_type=F32
    )
    return field[:total] + field[total:]


def observe(field, weights_ref, cell_ref, hits_ref, live, rows):
    levels, slots = weights_ref.shape
    chunk = 256
    high, low = split(field)
    both = jnp.concatenate([high, low], axis=1)
    observed = []
    for start in range(0, slots, chunk):
        hits = hits_ref[:, start : start + chunk]
        picked = dot(both, jnp.concatenate([hits, hits], axis=0))
        here = row_hits(cell_ref[:, start : start + chunk], rows, hits.shape[0])
        total = jnp.zeros((rows, chunk), F32)
        for level in range(levels):
            weight = weights_ref[level : level + 1, start : start + chunk]
            total = total + jnp.where(here, picked[level * rows : (level + 1) * rows], 0.0) * weight
        observed.append(jnp.sum(total, axis=0, keepdims=True))
    return jnp.concatenate(observed, axis=1) * live


def live_slots(count_ref, slots):
    return jnp.where(lax.broadcasted_iota(jnp.int32, (1, slots), 1) < count_ref[0], 1.0, 0.0)


def mix_rows(p_refs, g_refs, rows_matrix, mixed):
    total, columns = g_refs[0].shape
    for first in range(0, mixed.shape[0], 2):
        sides = []
        for member in (first, first + 1):
            sides.append(jnp.concatenate([p[member].astype(F32) * g[...] for p, g in zip(p_refs, g_refs)], axis=0))
        high, low = split(jnp.concatenate(sides, axis=1))
        product = dot(rows_matrix, high)
        high, low = split(product[:total] + product[total:] + dot(rows_matrix[:total], low))
        for i in range(2):
            lanes = slice(i * columns, (i + 1) * columns)
            mixed[first + i, :, :columns] = high[:, lanes]
            mixed[first + i, :, columns:] = low[:, lanes]


def across_columns(member, mixed, matrix):
    product = dot(mixed[member], matrix)
    columns = product.shape[1] // 2
    return product[:, :columns] + product[:, columns:]


def summed_members(field, weigh, p_side, g_side, constants, places, which, mixed):
    mix_rows([p_side], [g_side], constants[places[2, which]], mixed)
    for member in range(mixed.shape[0]):
        field = field + weigh[member].astype(F32) * across_columns(member, mixed, constants[places[2, "y"]])
    return field


def as_rows(line, width=128):
    return jnp.concatenate([line[:, i : i + width] for i in range(0, line.shape[1], width)], axis=0)


def as_line(block):
    return jnp.concatenate([block[i : i + 1] for i in range(block.shape[0])], axis=1)


def start_kernel(rows, columns, count, place, weights, cell, precision, innovations, field, precision_rows, c_rows, hits, parts):
    c = live_slots(count, weights.shape[1]) * precision[...] * innovations[...]
    hits[...] = column_hits(cell[...], columns)
    field[...] = adjoint(c, weights, cell, hits, rows, parts)
    precision_rows[...] = as_rows(precision[...])
    c_rows[...] = as_rows(c)


def own_kernel(places, p, g, constants, field, mixed):
    field[...] = summed_members(jnp.zeros(g.shape, F32), p, p, g, constants, places, "o", mixed)


def side_kernel(places, p, p_side, g_side, part, constants, field, mixed):
    field[...] = summed_members(part[...], p, p_side, g_side, constants, places, "a", mixed)


def message_rows(place, observed, field, kept, given):
    lines = observed.shape[0]
    half = field.shape[0] // CORES
    core = lax.rem(place[0], CORES)
    for message, at in ((kept, core), (given, 1 - core)):
        message[:lines] = observed
        message[lines:] = field[pl.ds(pl.multiple_of(at * half, half), half)]


def observe_kernel(rows, places, count, place, p, p_side, g_side, part, constants, weights, cell, hits, kept, given, field, mixed):
    field[...] = summed_members(part[...], p, p_side, g_side, constants, places, "b", mixed)
    observed = as_rows(observe(field[...], weights, cell, hits, live_slots(count, weights.shape[1]), rows))
    message_rows(place, observed, field, kept, given)


def sum_kernel(first, second, total):
    total[...] = first[...] + second[...]


def middle_kernel(rows, count, *refs):
    *messages, weights, cell, hits, precision, after, field, observed, half, parts = refs
    lines = observed.shape[0]
    half[...] = sum(message[lines:] for message in messages)
    summed = sum(message[:lines] for message in messages)
    observed[...] = summed
    field[...] = adjoint(precision[...] * as_line(summed), weights, cell, hits, rows, parts)


def alpha_kernel(places, p0, p1, p2, g0, g1, g2, constants, after, alpha, token, mixed):
    matrix = jnp.concatenate([constants[places[1, name]] for name in "boa"], axis=1)
    mix_rows((p0, p1, p2), (g0, g1, g2), matrix, mixed)
    for member in range(mixed.shape[0]):
        alpha[member] = across_columns(member, mixed, constants[places[1, "y"]])
    token[...] = jnp.zeros(token.shape, F32)


def scalars_kernel(*refs):
    *messages, once, half0, precision, c_rows, after, scalars, halves = refs
    lines = once.shape[0]
    z2 = sum(message[:lines] for message in messages)
    halves[0] = half0[...]
    halves[1] = sum(message[lines:] for message in messages)
    z1 = once[...]
    rho = precision[...]
    c = c_rows[...]

    def total(x):
        return jnp.sum(jnp.sum(x, axis=0, keepdims=True), axis=1, keepdims=True)

    d = c + rho * z1
    e = z1 + z2
    size = total(d * d)
    shift = jnp.where(size > 0.0, total(c * d) / jnp.where(size > 0.0, size, 1.0), 0.0)
    shift = jnp.clip(shift, 0.0, 1.0)
    v = c - shift * d
    w = z1 - shift * e
    values = [
        shift,
        total(c * z1),
        total(d * z1),
        total(v * w),
        total(v * e + d * w),
        total(d * e),
        total(v * z1 + c * w),
        total(d * z1 + c * e),
        total(rho * w * w),
        total(rho * w * e),
        total(rho * e * e),
        total(rho * w * z1),
        total(rho * e * z1),
        total(rho * z1 * z1),
    ]
    lane = lax.broadcasted_iota(jnp.int32, (1, scalars.shape[1]), 1)
    line = jnp.zeros((1, scalars.shape[1]), F32)
    for i, value in enumerate(values):
        line = jnp.where(lane == i, value, line)
    scalars[...] = jnp.broadcast_to(line, scalars.shape)


def combination(scalars):
    table = scalars[...]

    def column(i):
        return table[:, i : i + 1]

    def total(x):
        return jnp.sum(x, axis=0, keepdims=True)

    cz = total(column(1))
    step0 = cz / total(column(2))
    delta = step0 - column(0)
    rr1 = total(column(3) - delta * column(4) + delta * delta * column(5))
    beta = rr1 / cz
    pq1 = rr1 + beta * total(column(6) - delta * column(7)) + beta * beta * cz
    pq1 = pq1 + total(column(8) - 2.0 * delta * column(9) + delta * delta * column(10))
    pq1 = pq1 + 2.0 * beta * total(column(11) - delta * column(12)) + beta * beta * total(column(13))
    step1 = rr1 / pq1
    return step0 + step1 * (1.0 - step0 + beta), -step1 * step0


def final_kernel(place, scalars, alpha0, alpha1, mine, other, alpha_out, increment_out, alpha, increment, sems):
    first, second = combination(scalars)
    core = lax.rem(place[0], CORES)
    half = mine.shape[1]
    for part, at in ((mine, core), (other, 1 - core)):
        increment[pl.ds(pl.multiple_of(at * half, half), half)] = first * part[0] + second * part[1]
    copies = [pltpu.make_async_copy(increment, increment_out, sems.at[0])]
    copies[0].start()
    for member in range(0, alpha.shape[0], 2):
        pair = pl.ds(member, 2)
        alpha[pair] = first * alpha0[pair] + second * alpha1[pair]
        copies.append(pltpu.make_async_copy(alpha.at[pair], alpha_out.at[pair], sems.at[1 + member // 2]))
        copies[-1].start()
    for copy in copies:
        copy.wait()


def in_vmem(x):
    return x, pl.BlockSpec(memory_space=pltpu.VMEM)


def in_smem(x):
    return x, pl.BlockSpec(memory_space=pltpu.SMEM)


def anywhere(x):
    return x, pl.BlockSpec(memory_space=pl.ANY)


def call(kernel, outs, args, scratch=(), out_space=pltpu.VMEM):
    single = not isinstance(outs, list)
    outs = [outs] if single else outs
    shapes = [out if isinstance(out, jax.ShapeDtypeStruct) else jax.ShapeDtypeStruct(out, F32) for out in outs]
    out_spec = pl.BlockSpec(memory_space=out_space)
    return pl.pallas_call(
        kernel,
        out_shape=shapes[0] if single else shapes,
        in_specs=[spec for _, spec in args],
        out_specs=out_spec if single else [out_spec] * len(shapes),
        scratch_shapes=list(scratch),
        compiler_params=pltpu.CompilerParams(vmem_limit_bytes=VMEM_LIMIT),
    )(*[x for x, _ in args])


def neighbours(x):
    size = lax.axis_size("tile")
    up = [(i, (i + 1) % size) for i in range(size)]
    down = [(j, i) for i, j in up]
    return lax.ppermute(x, "tile", up), lax.ppermute(x, "tile", down)


def local(perturbations, innovations, obs_precision, obs_weights, obs_cell, obs_count):
    members, levels, rows, columns = perturbations.shape
    slots = obs_cell.shape[0]
    cells = levels * rows
    ens, tiles = lax.axis_size("ens"), lax.axis_size("tile")
    constants = Constants(levels, rows, columns, ens * members)
    places = constants.places
    constants = jnp.asarray(constants.array)
    lines = slots // 128
    p = perturbations.reshape(members, cells, columns)
    cell = obs_cell.reshape(1, slots)
    precision = obs_precision.reshape(1, slots)
    innovations_line = innovations.reshape(1, slots)
    shape = (rows, columns)

    def bound(kernel, *values):
        def run(*refs):
            kernel(*values, *refs)

        return run

    field_shape = (cells, columns)
    half = cells // CORES
    chips = ens // CORES
    place = lax.axis_index("ens").reshape(1)
    vmem = lambda *xs: [in_vmem(x) for x in xs]

    mixed = pltpu.VMEM((members, cells, 2 * columns), BF16)

    def own_and_after(g, g_after):
        part = call(bound(own_kernel, places), field_shape, vmem(p, g, constants), [mixed])
        return call(bound(side_kernel, places), field_shape, vmem(p, p_after, g_after, part, constants), [mixed])

    def other_core(x):
        return lax.ppermute(x, "ens", [(i, i ^ 1) for i in range(ens)])

    def from_chips(x):
        arrived = [x]
        for back in range(1, chips):
            route = [(c * CORES + core, (c + back) % chips * CORES + core) for c in range(chips) for core in range(CORES)]
            arrived.append(lax.ppermute(x, "ens", route))
        return arrived

    def summed(first, second):
        return call(sum_kernel, first.shape, vmem(first, second))

    def alpha_of(g, g_before, g_after, after):
        return call(
            bound(alpha_kernel, places), [(members, cells, columns), (8, 128)],
            vmem(p_before, p, p_after, g_before, g, g_after, constants) + [anywhere(after)], [mixed],
        )

    p_before, p_after = neighbours(p)
    weights = obs_weights
    parts = pltpu.VMEM((2 * cells, slots), BF16)
    g0, precision_rows, c_rows, hits = call(
        bound(start_kernel, *shape),
        [field_shape, (lines, 128), (lines, 128), jax.ShapeDtypeStruct((columns, slots), BF16)],
        [in_smem(obs_count), in_smem(place)] + vmem(weights, cell, precision, innovations_line), [parts],
    )
    g0_before, g0_after = neighbours(g0)
    part = own_and_after(g0, g0_after)
    message = (lines + half, columns)
    kept, given = call(
        bound(observe_kernel, rows, places), [message, message],
        [in_smem(obs_count), in_smem(place)] + vmem(p, p_before, g0_before, part, constants, weights, cell, hits),
        [pltpu.VMEM(field_shape, F32), mixed],
    )
    sent = summed(kept, other_core(given))
    messages = from_chips(sent)
    alpha0, done0 = alpha_of(g0, g0_before, g0_after, sent)
    g1, once, half0 = call(
        bound(middle_kernel, rows), [field_shape, (lines, 128), (half, columns)],
        [in_smem(obs_count)] + vmem(*messages, weights, cell, hits, precision) + [anywhere(done0)],
        [parts],
    )
    g1_before, g1_after = neighbours(g1)
    part = own_and_after(g1, g1_after)
    kept, given = call(
        bound(observe_kernel, rows, places), [message, message],
        [in_smem(obs_count), in_smem(place)] + vmem(p, p_before, g1_before, part, constants, weights, cell, hits),
        [pltpu.VMEM(field_shape, F32), mixed],
    )
    sent = summed(kept, other_core(given))
    messages = from_chips(sent)
    alpha1, done1 = alpha_of(g1, g1_before, g1_after, sent)
    scalars, mine = call(
        scalars_kernel, [(tiles, 128), (2, half, columns)],
        vmem(*messages, once, half0, precision_rows, c_rows) + [anywhere(done1)],
    )
    other = other_core(mine)
    scalars = lax.all_to_all(scalars.reshape(tiles, 1, 128), "tile", 0, 0).reshape(tiles, 128)
    alpha, increment = call(
        final_kernel, [(members, cells, columns), field_shape],
        [in_smem(place)] + vmem(scalars, alpha0, alpha1, mine, other),
        [pltpu.VMEM((members, cells, columns), F32), pltpu.VMEM(field_shape, F32), pltpu.SemaphoreType.DMA((members,))],
        out_space=pl.ANY,
    )
    return alpha.reshape(perturbations.shape), increment.reshape(levels, rows, columns)


def solution(mesh):
    placed = (
        P("ens", None, "tile", None),
        P("tile"),
        P("tile"),
        P(None, "tile"),
        P("tile"),
        P("tile"),
    )
    return jax.shard_map(
        local,
        mesh=mesh,
        in_specs=placed,
        out_specs=(P("ens", None, "tile", None), P(None, "tile", None)),
        check_vma=False,
    )
```

```python
import math

import jax
import jax.numpy as jnp
import numpy as np
from jax import lax
from jax.experimental import pallas as pl
from jax.experimental.pallas import tpu as pltpu
from jax.sharding import PartitionSpec as P

F32 = jnp.float32
BF16 = jnp.bfloat16
VERTICAL_SPREAD = 2.0
CORES = 2
VMEM_LIMIT = 12 * 1024 * 1024


def gauss(radius, spread):
    offsets = np.arange(-radius, radius + 1) / spread
    return np.exp(-offsets * offsets)


def band(length, spread):
    position = np.arange(length)
    spacing = (position[:, None] - position[None, :]) / spread
    return np.exp(-spacing * spacing) / np.sqrt(np.sum(gauss(length, spread) ** 2))


def bf16_pair(matrix):
    matrix = matrix.astype(np.float32)
    high = matrix.astype(jnp.bfloat16)
    low = (matrix - high.astype(np.float32)).astype(jnp.bfloat16)
    return high, low


def local_matrices(levels, rows, columns, power, scale):
    radius = rows // 2
    kernel = gauss(radius, float(radius))
    kernel = kernel / np.sqrt(np.sum(kernel * kernel))
    vertical = band(levels, VERTICAL_SPREAD)
    lateral = band(columns, columns / 16.0)
    if power == 2:
        kernel = np.convolve(kernel, kernel)
        vertical = vertical @ vertical
        lateral = lateral @ lateral
    reach = (len(kernel) - 1) // 2
    blocks = []
    for tile in (-1, 0, 1):
        offset = tile * rows + np.arange(rows)[None, :] - np.arange(rows)[:, None]
        inside = np.abs(offset) <= reach
        along = np.where(inside, kernel[np.clip(offset + reach, 0, 2 * reach)], 0.0)
        blocks.append(np.concatenate(bf16_pair(np.kron(vertical, along) * scale)))
    high, low = bf16_pair(lateral)
    return blocks, np.block([[high, low], [high, np.zeros_like(low)]])


class Constants:
    def __init__(self, levels, rows, columns, members):
        self.places, arrays, start = {}, [], 0
        for power in (2, 1):
            blocks, across = local_matrices(levels, rows, columns, power, float(members) ** (-power / 2))
            for name, array in list(zip("boa", blocks)) + [("y", across)]:
                self.places[power, name] = slice(start, start + array.shape[0])
                arrays.append(array)
                start += array.shape[0]
        self.array = np.concatenate(arrays)


def split(x):
    high = x.astype(BF16)
    return high, (x - high.astype(F32)).astype(BF16)


def dot(a, b):
    return jnp.dot(a, b, preferred_element_type=F32)


def column_hits(cell, columns):
    return jnp.where(
        lax.broadcasted_iota(jnp.int32, (columns, cell.shape[1]), 0) == cell % columns, 1.0, 0.0
    ).astype(BF16)


def adjoint(values, weights_ref, cell_ref, rows, columns):
    levels, slots = weights_ref.shape
    total = levels * rows
    chunk = 256
    field = jnp.zeros((2 * total, columns), F32)
    for start in range(0, slots, chunk):
        cell = cell_ref[:, start : start + chunk]
        hits = column_hits(cell, columns)
        here = lax.broadcasted_iota(jnp.int32, (rows, chunk), 0) == cell // columns
        weighted = weights_ref[:, start : start + chunk] * values[:, start : start + chunk]
        parts = [jnp.where(here, weighted[level : level + 1], 0.0) for level in range(levels)]
        high, low = split(jnp.concatenate(parts, axis=0))
        both = jnp.concatenate([high, low], axis=0)
        field = field + lax.dot_general(both, hits, (((1,), (1,)), ((), ())), preferred_element_type=F32)
    return field[:total] + field[total:]


def observe(field, weights_ref, cell_ref, live, rows, columns):
    levels, slots = weights_ref.shape
    chunk = 256
    high, low = split(field)
    both = jnp.concatenate([high, low], axis=1)
    observed = []
    for start in range(0, slots, chunk):
        cell = cell_ref[:, start : start + chunk]
        hits = column_hits(cell, columns)
        picked = dot(both, jnp.concatenate([hits, hits], axis=0))
        here = lax.broadcasted_iota(jnp.int32, (rows, chunk), 0) == cell // columns
        total = jnp.zeros((rows, chunk), F32)
        for level in range(levels):
            weight = weights_ref[level : level + 1, start : start + chunk]
            total = total + jnp.where(here, picked[level * rows : (level + 1) * rows], 0.0) * weight
        observed.append(jnp.sum(total, axis=0, keepdims=True))
    return jnp.concatenate(observed, axis=1) * live


def live_slots(count_ref, slots):
    return jnp.where(lax.broadcasted_iota(jnp.int32, (1, slots), 1) < count_ref[0], 1.0, 0.0)


def mix_rows(p_refs, g_refs, rows_matrix, mixed):
    total, columns = g_refs[0].shape
    for first in range(0, mixed.shape[0], 2):
        sides = []
        for member in (first, first + 1):
            sides.append(jnp.concatenate([p[member].astype(F32) * g[...] for p, g in zip(p_refs, g_refs)], axis=0))
        high, low = split(jnp.concatenate(sides, axis=1))
        product = dot(rows_matrix, high)
        high, low = split(product[:total] + product[total:] + dot(rows_matrix[:total], low))
        for i in range(2):
            lanes = slice(i * columns, (i + 1) * columns)
            mixed[first + i, :, :columns] = high[:, lanes]
            mixed[first + i, :, columns:] = low[:, lanes]


def across_columns(member, mixed, matrix):
    product = dot(mixed[member], matrix)
    columns = product.shape[1] // 2
    return product[:, :columns] + product[:, columns:]


def summed_members(field, weigh, p_side, g_side, constants, places, which, mixed):
    mix_rows([p_side], [g_side], constants[places[2, which]], mixed)
    for member in range(mixed.shape[0]):
        field = field + weigh[member].astype(F32) * across_columns(member, mixed, constants[places[2, "y"]])
    return field


def as_rows(line, width=128):
    return jnp.concatenate([line[:, i : i + width] for i in range(0, line.shape[1], width)], axis=0)


def as_line(block):
    return jnp.concatenate([block[i : i + 1] for i in range(block.shape[0])], axis=1)


def start_kernel(rows, columns, count, place, weights, cell, precision, innovations, field, precision_rows, c_rows):
    c = live_slots(count, weights.shape[1]) * precision[...] * innovations[...]
    field[...] = adjoint(c, weights, cell, rows, columns)
    precision_rows[...] = as_rows(precision[...])
    c_rows[...] = as_rows(c)


def own_kernel(places, p, g, constants, field, mixed):
    field[...] = summed_members(jnp.zeros(g.shape, F32), p, p, g, constants, places, "o", mixed)


def side_kernel(places, which, p, p_side, g_side, part, constants, field, mixed):
    field[...] = summed_members(part[...], p, p_side, g_side, constants, places, which, mixed)


def message_rows(place, observed, field, kept, given):
    lines = observed.shape[0]
    half = field.shape[0] // CORES
    core = lax.rem(place[0], CORES)
    for message, at in ((kept, core), (given, 1 - core)):
        message[:lines] = observed
        message[lines:] = field[pl.ds(pl.multiple_of(at * half, half), half)]


def observe_kernel(rows, columns, places, which, count, place, p, p_side, g_side, part, constants, weights, cell, kept, given, field, mixed):
    field[...] = summed_members(part[...], p, p_side, g_side, constants, places, which, mixed)
    observed = as_rows(observe(field[...], weights, cell, live_slots(count, weights.shape[1]), rows, columns))
    message_rows(place, observed, field, kept, given)


def sum_kernel(first, second, total):
    total[...] = first[...] + second[...]


def middle_kernel(rows, columns, count, *refs):
    *messages, weights, cell, precision, after, field, observed, half = refs
    lines = observed.shape[0]
    half[...] = sum(message[lines:] for message in messages)
    summed = sum(message[:lines] for message in messages)
    observed[...] = summed
    field[...] = adjoint(precision[...] * as_line(summed), weights, cell, rows, columns)


def alpha_kernel(places, p0, p1, p2, g0, g1, g2, constants, after, alpha, token, mixed):
    matrix = jnp.concatenate([constants[places[1, name]] for name in "boa"], axis=1)
    mix_rows((p0, p1, p2), (g0, g1, g2), matrix, mixed)
    for member in range(mixed.shape[0]):
        alpha[member] = across_columns(member, mixed, constants[places[1, "y"]])
    token[...] = jnp.zeros(token.shape, F32)


def scalars_kernel(*refs):
    *messages, once, half0, precision, c_rows, after, scalars, halves = refs
    lines = once.shape[0]
    z2 = sum(message[:lines] for message in messages)
    halves[0] = half0[...]
    halves[1] = sum(message[lines:] for message in messages)
    z1 = once[...]
    rho = precision[...]
    c = c_rows[...]

    def total(x):
        return jnp.sum(jnp.sum(x, axis=0, keepdims=True), axis=1, keepdims=True)

    d = c + rho * z1
    e = z1 + z2
    size = total(d * d)
    shift = jnp.where(size > 0.0, total(c * d) / jnp.where(size > 0.0, size, 1.0), 0.0)
    shift = jnp.clip(shift, 0.0, 1.0)
    v = c - shift * d
    w = z1 - shift * e
    values = [
        shift,
        total(c * z1),
        total(d * z1),
        total(v * w),
        total(v * e + d * w),
        total(d * e),
        total(v * z1 + c * w),
        total(d * z1 + c * e),
        total(rho * w * w),
        total(rho * w * e),
        total(rho * e * e),
        total(rho * w * z1),
        total(rho * e * z1),
        total(rho * z1 * z1),
    ]
    lane = lax.broadcasted_iota(jnp.int32, (1, scalars.shape[1]), 1)
    line = jnp.zeros((1, scalars.shape[1]), F32)
    for i, value in enumerate(values):
        line = jnp.where(lane == i, value, line)
    scalars[...] = jnp.broadcast_to(line, scalars.shape)


def combination(scalars):
    table = scalars[...]

    def column(i):
        return table[:, i : i + 1]

    def total(x):
        return jnp.sum(x, axis=0, keepdims=True)

    cz = total(column(1))
    step0 = cz / total(column(2))
    delta = step0 - column(0)
    rr1 = total(column(3) - delta * column(4) + delta * delta * column(5))
    beta = rr1 / cz
    pq1 = rr1 + beta * total(column(6) - delta * column(7)) + beta * beta * cz
    pq1 = pq1 + total(column(8) - 2.0 * delta * column(9) + delta * delta * column(10))
    pq1 = pq1 + 2.0 * beta * total(column(11) - delta * column(12)) + beta * beta * total(column(13))
    step1 = rr1 / pq1
    return step0 + step1 * (1.0 - step0 + beta), -step1 * step0


def final_kernel(place, scalars, alpha0, alpha1, mine, other, alpha_out, increment_out, alpha, increment, sems):
    first, second = combination(scalars)
    core = lax.rem(place[0], CORES)
    half = mine.shape[1]
    for part, at in ((mine, core), (other, 1 - core)):
        increment[pl.ds(pl.multiple_of(at * half, half), half)] = first * part[0] + second * part[1]
    copies = [pltpu.make_async_copy(increment, increment_out, sems.at[0])]
    copies[0].start()
    for member in range(0, alpha.shape[0], 2):
        pair = pl.ds(member, 2)
        alpha[pair] = first * alpha0[pair] + second * alpha1[pair]
        copies.append(pltpu.make_async_copy(alpha.at[pair], alpha_out.at[pair], sems.at[1 + member // 2]))
        copies[-1].start()
    for copy in copies:
        copy.wait()


def in_vmem(x):
    return x, pl.BlockSpec(memory_space=pltpu.VMEM)


def in_smem(x):
    return x, pl.BlockSpec(memory_space=pltpu.SMEM)


def anywhere(x):
    return x, pl.BlockSpec(memory_space=pl.ANY)


def call(kernel, outs, args, scratch=(), out_space=pltpu.VMEM):
    single = not isinstance(outs, list)
    shapes = [jax.ShapeDtypeStruct(shape, F32) for shape in ([outs] if single else outs)]
    out_spec = pl.BlockSpec(memory_space=out_space)
    return pl.pallas_call(
        kernel,
        out_shape=shapes[0] if single else shapes,
        in_specs=[spec for _, spec in args],
        out_specs=out_spec if single else [out_spec] * len(shapes),
        scratch_shapes=list(scratch),
        compiler_params=pltpu.CompilerParams(vmem_limit_bytes=VMEM_LIMIT),
    )(*[x for x, _ in args])


def neighbours(x):
    size = lax.axis_size("tile")
    up = [(i, (i + 1) % size) for i in range(size)]
    down = [(j, i) for i, j in up]
    return lax.ppermute(x, "tile", up), lax.ppermute(x, "tile", down)


def local(perturbations, innovations, obs_precision, obs_weights, obs_cell, obs_count):
    members, levels, rows, columns = perturbations.shape
    slots = obs_cell.shape[0]
    cells = levels * rows
    ens, tiles = lax.axis_size("ens"), lax.axis_size("tile")
    constants = Constants(levels, rows, columns, ens * members)
    places = constants.places
    constants = jnp.asarray(constants.array)
    lines = slots // 128
    p = perturbations.reshape(members, cells, columns)
    cell = obs_cell.reshape(1, slots)
    precision = obs_precision.reshape(1, slots)
    innovations_line = innovations.reshape(1, slots)
    shape = (rows, columns)

    def bound(kernel, *values):
        def run(*refs):
            kernel(*values, *refs)

        return run

    field_shape = (cells, columns)
    half = cells // CORES
    chips = ens // CORES
    place = lax.axis_index("ens").reshape(1)
    vmem = lambda *xs: [in_vmem(x) for x in xs]

    mixed = pltpu.VMEM((members, cells, 2 * columns), BF16)

    def own_and_side(which, g, p_side, g_side):
        part = call(bound(own_kernel, places), field_shape, vmem(p, g, constants), [mixed])
        return call(bound(side_kernel, places, which), field_shape, vmem(p, p_side, g_side, part, constants), [mixed])

    def other_core(x):
        return lax.ppermute(x, "ens", [(i, i ^ 1) for i in range(ens)])

    def from_chips(x):
        arrived = [x]
        for back in range(1, chips):
            route = [(c * CORES + core, (c + back) % chips * CORES + core) for c in range(chips) for core in range(CORES)]
            arrived.append(lax.ppermute(x, "ens", route))
        return arrived

    def summed(first, second):
        return call(sum_kernel, first.shape, vmem(first, second))

    def alpha_of(g, g_before, g_after, after):
        return call(
            bound(alpha_kernel, places), [(members, cells, columns), (8, 128)],
            vmem(p_before, p, p_after, g_before, g, g_after, constants) + [anywhere(after)], [mixed],
        )

    p_before, p_after = neighbours(p)
    weights = obs_weights
    g0, precision_rows, c_rows = call(
        bound(start_kernel, *shape), [field_shape, (lines, 128), (lines, 128)],
        [in_smem(obs_count), in_smem(place)] + vmem(weights, cell, precision, innovations_line),
    )
    g0_before, g0_after = neighbours(g0)
    part = own_and_side("b", g0, p_before, g0_before)
    message = (lines + half, columns)
    kept, given = call(
        bound(observe_kernel, *shape, places, "a"), [message, message],
        [in_smem(obs_count), in_smem(place)] + vmem(p, p_after, g0_after, part, constants, weights, cell),
        [pltpu.VMEM(field_shape, F32), mixed],
    )
    sent = summed(kept, other_core(given))
    messages = from_chips(sent)
    alpha0, done0 = alpha_of(g0, g0_before, g0_after, sent)
    g1, once, half0 = call(
        bound(middle_kernel, *shape), [field_shape, (lines, 128), (half, columns)],
        [in_smem(obs_count)] + vmem(*messages, weights, cell, precision) + [anywhere(done0)],
    )
    g1_before, g1_after = neighbours(g1)
    part = own_and_side("b", g1, p_before, g1_before)
    kept, given = call(
        bound(observe_kernel, *shape, places, "a"), [message, message],
        [in_smem(obs_count), in_smem(place)] + vmem(p, p_after, g1_after, part, constants, weights, cell),
        [pltpu.VMEM(field_shape, F32), mixed],
    )
    sent = summed(kept, other_core(given))
    messages = from_chips(sent)
    alpha1, done1 = alpha_of(g1, g1_before, g1_after, sent)
    scalars, mine = call(
        scalars_kernel, [(tiles, 128), (2, half, columns)],
        vmem(*messages, once, half0, precision_rows, c_rows) + [anywhere(done1)],
    )
    other = other_core(mine)
    scalars = lax.all_to_all(scalars.reshape(tiles, 1, 128), "tile", 0, 0).reshape(tiles, 128)
    alpha, increment = call(
        final_kernel, [(members, cells, columns), field_shape],
        [in_smem(place)] + vmem(scalars, alpha0, alpha1, mine, other),
        [pltpu.VMEM((members, cells, columns), F32), pltpu.VMEM(field_shape, F32), pltpu.SemaphoreType.DMA((members,))],
        out_space=pl.ANY,
    )
    return alpha.reshape(perturbations.shape), increment.reshape(levels, rows, columns)


def solution(mesh):
    placed = (
        P("ens", None, "tile", None),
        P("tile"),
        P("tile"),
        P(None, "tile"),
        P("tile"),
        P("tile"),
    )
    return jax.shard_map(
        local,
        mesh=mesh,
        in_specs=placed,
        out_specs=(P("ens", None, "tile", None), P(None, "tile", None)),
        check_vma=False,
    )
```
